128 devices in a mesh: row: 8 (over y, core), col: 16 (over x, z).
Axes of the slice: x: 4, y: 4, z: 4, core: 2. Of those that a mesh axis runs over, the one named last changes fastest.
Arguments:
- rhs_tile: float32 [18432, 18432], P('row', 'col'), may hold values from -6 to 6
- factor: float32 [18432, 1536], P('row', 'col'), may hold values from -1 to 2.5, as said below
Outputs:
- whitened: float32 [18432, 18432], P('row', 'col')
The draws below stay inside these ranges and needn't reach their ends.
Inputs may be any that keep to these rules, and one draw needn't show every extreme that they name: In elimination order factor is lower triangular: entries above the diagonal are zero, diagonal entries are at least 0.7.
All inputs are finite; a program needn't handle non-finite values.
Results may differ from the reference program's by a relative error of at most 0.0001.
Values sent between devices are 32-bit elements; how exact they have to be, the bound alone decides.
No kernel may reach another device: no remote copies, remote signals or barrier semaphores. Data moves between devices by JAX's collectives and lax.ppermute only.
A program may use at most 128 MiB of HBM per device.

```python
import jax
import jax.numpy as jnp
from jax import lax

N = 18432
PANEL = 512
PANELS = 3
ROWS_DEV = 2304
PB = 64
CB = 32
NRHS = 18432


def draw_factor(key, part):
    window = PANELS * PANEL
    stored = jnp.arange(N).astype(jnp.int32)[:, None]
    column = jnp.arange(window).astype(jnp.int32)[None, :]
    local_row = stored % ROWS_DEV
    stored_panel = local_row // PB
    row_rank = jnp.where(stored_panel < PANELS, stored_panel * PANEL + stored // ROWS_DEV * PB + local_row % PB, window + local_row)
    col_owner = column // (PANELS * CB)
    col_local = column % (PANELS * CB)
    col_panel = col_local // CB
    col_rank = col_panel * PANEL + col_owner * CB + col_local % CB
    key_noise = jax.random.fold_in(key, 11)
    key_diag = jax.random.fold_in(key, 23)
    normal_draw = jnp.clip(jax.random.normal(key_noise, (N, window), jnp.float32), -6.0, 6.0)
    diag_vals = jax.random.uniform(key_diag, (N, window), jnp.float32, 1.0, 2.0)
    near_scale = 0.5
    far_scale = 1.0
    same_panel = row_rank // PANEL == col_panel
    lower_vals = jnp.where(same_panel, normal_draw * (near_scale / jnp.sqrt(1.0 * PANEL)), normal_draw * (far_scale / jnp.sqrt(1.0 * window)))
    values = jnp.where(row_rank == col_rank, diag_vals, jnp.where(row_rank > col_rank, lower_vals, 0.0))
    return values.astype(jnp.float32)


def shard_levels(rng, extent, pieces, smallest, largest):
    def one(dim, blocks):
        steps = jax.random.uniform(jax.random.fold_in(jax.random.fold_in(rng, 6), dim), (blocks,), jnp.float32, smallest / len(pieces), largest / len(pieces))
        return jnp.repeat(jnp.exp(steps), extent[dim] // blocks).reshape((-1,) + (1,) * (len(extent) - dim - 1))

    level = one(*pieces[0])
    for cut in pieces[1:]:
        level = level * one(*cut)
    return level


def bell_draw(key, dims, deviation, limit, shards=(), kind=jnp.bfloat16):
    values = deviation * jax.random.normal(key, dims, jnp.float32)
    if shards:
        values = values * shard_levels(key, dims, shards, -0.22, 0.18)
    return jnp.clip(values, -limit, limit).astype(kind)


def setup_inputs(seed: int = 0) -> dict:
    key_of = jax.random.split(jax.random.key(seed), 3)
    rhs_tile = bell_draw(key_of[0], (N, NRHS), 1.0, 6.0, ((0, 8), (1, 16)), jnp.float32)
    factor = draw_factor(jax.random.fold_in(key_of[2], 71), 0)
    return {"rhs_tile": rhs_tile, "factor": factor}


def reference(rhs_tile, factor):
    window = PANELS * PANEL
    index_k = jnp.arange(window).astype(jnp.int32)
    panel_of = index_k // PANEL
    within = index_k % PANEL
    rows_index = (within // PB * ROWS_DEV + panel_of * PB + within % PB).astype(jnp.int32)
    cols_index = (within // CB * (PANELS * CB) + panel_of * CB + within % CB).astype(jnp.int32)
    factor_cols = factor[:, cols_index]
    stored = jnp.arange(N).astype(jnp.int32)
    local_row = stored % ROWS_DEV
    stored_panel = local_row // PB
    order_rank = jnp.where(stored_panel < PANELS, stored_panel * PANEL + stored // ROWS_DEV * PB + local_row % PB, window)
    result = rhs_tile
    for panel_index in range(PANELS):
        start_row = panel_index * PANEL
        end_row = start_row + PANEL
        panel_rows = rows_index[start_row:end_row]
        diagonal = factor_cols[panel_rows][:, start_row:end_row]
        solved = jax.scipy.linalg.solve_triangular(diagonal, result[panel_rows], lower=True)
        update = jnp.dot(factor_cols[:, start_row:end_row].astype(jnp.float32), solved.astype(jnp.float32), precision=lax.Precision.HIGHEST, preferred_element_type=jnp.float32)
        result = jnp.where((order_rank >= end_row)[:, None], result - update, result)
        result = result.at[panel_rows].set(solved)
    return result
```

```python
import jax
import jax.numpy as jnp
from jax import lax
from jax.experimental import pallas as pl
from jax.experimental.pallas import tpu as pltpu
from jax.sharding import PartitionSpec as P

F32, BF16 = jnp.float32, jnp.bfloat16
NX, NY, NZ = 4, 4, 4
ROWS, NCOL = 2304, 1152
PB, CB, PANEL, PANELS = 64, 32, 512, 3
WIN = PB * PANELS
TRAIL = ROWS - WIN
GROUPS = 4
GR = TRAIL // GROUPS
SLOTS = 6
MIB = 1024 * 1024
GROUP_ORDER = (0, 1, 3, 2)


def joint(v, dest):
    pairs = []
    for y in range(NY):
        for c in range(2):
            for x in range(NX):
                for z in range(NZ):
                    ty, tc, tx, tz = dest(y, c, x, z)
                    pairs.append(
                        (
                            (y * 2 + c) * 16 + x * 4 + z,
                            ((ty % NY) * 2 + tc % 2) * 16 + (tx % NX) * 4 + tz % NZ,
                        )
                    )
    return lax.ppermute(v, ("row", "col"), pairs)


def from_first(v, d):
    return joint(v, lambda y, c, x, z: (y, c, x - d, z) if c == 0 else (y, c, x, z - d))


def from_second(v, d):
    return joint(v, lambda y, c, x, z: (y, c, x, z - d) if c == 0 else (y, c, x - d, z))


def from_y(v, d):
    return joint(v, lambda y, c, x, z: (y - d, c, x, z))


def from_core(v):
    return joint(v, lambda y, c, x, z: (y, 1 - c, x, z))


def pack_kernel(f_ref, l_ref, w_ref):
    for p in range(PANELS):
        l_ref[p * GR : (p + 1) * GR, :] = jnp.concatenate(
            [
                f_ref[WIN + g * GR : WIN + (g + 1) * GR, p * CB : (p + 1) * CB]
                for g in range(GROUPS)
            ],
            axis=1,
        )

    def block(i, j):
        return f_ref[i * PB : (i + 1) * PB, j * CB : (j + 1) * CB]

    w_ref[0:PB, :] = jnp.concatenate([block(0, 0), block(1, 1), block(2, 2), block(1, 0)], axis=1)
    zero = jnp.zeros((PB, CB), F32)
    w_ref[PB : 2 * PB, :] = jnp.concatenate([block(2, 0), block(2, 1), zero, zero], axis=1)


def source(pos, i, j):
    core, x, z = pos[1], pos[2], pos[3]
    xs = jnp.where(core == 0, x + j, x + i) % NX
    zs = jnp.where(core == 0, z + i, z + j) % NZ
    return xs * NZ + zs


def rows_kernel(pos, g0, g1, g2, g3, out, canon):
    y, core = pos[0], pos[1]
    for i, ref in enumerate((g0, g1, g2, g3)):
        for j in range(4):
            canon[source(pos, i, j)] = ref[j]
    lane = lax.broadcasted_iota(jnp.int32, (PB, 128), 1)
    row = lax.broadcasted_iota(jnp.int32, (PB, 128), 0)
    for s in range(SLOTS):
        half, q = divmod(s, 4)
        for xs in range(NX):
            total = None
            for zs in range(NZ):
                v = canon[xs * NZ + zs, half * PB : (half + 1) * PB, :]
                shift = (zs - q) % 4 * CB
                v = pltpu.roll(v, shift, 1) if shift else v
                total = v if total is None else jnp.where(lane // CB == zs, v, total)
            out[s * 4 + xs] = total
    eye = (lane == row).astype(F32)
    blocks, mats, sols = [], [], []
    for p in range(PANELS):
        blk = out[p * 4 + y]
        blocks.append(blk)
        a = jnp.where(core == 1, pltpu.roll(blk, PB, 1), blk)
        mats.append((a, a - eye))
        sols.append([eye[8 * k : 8 * k + 8] for k in range(PB // 8)])
    for i in range(PB):
        for p in range(PANELS):
            a, am = mats[p]
            k0, r0 = divmod(i, 8)
            top = sols[p][k0][r0 : r0 + 1, :] * (1.0 / a[i : i + 1, i : i + 1])
            for k in range(k0, PB // 8):
                sols[p][k] = sols[p][k] - am[8 * k : 8 * k + 8, i : i + 1] * top
    for p in range(PANELS):
        inv = jnp.concatenate(sols[p], axis=0)
        inv = jnp.where(core == 1, pltpu.roll(inv, PB, 1), inv)
        out[p * 4 + y] = jnp.where(lane // PB == core, inv, blocks[p])


def exact_dot(a, b):
    return jnp.dot(a, b, precision=lax.Precision.HIGHEST, preferred_element_type=F32)


def split(v):
    hi = v.astype(BF16)
    return hi, (v - hi.astype(F32)).astype(BF16)


def dot3(ah, al, bh, bl):
    def d(a, b):
        return jnp.dot(a, b, preferred_element_type=F32)

    return d(ah, bh) + (d(ah, bl) + d(al, bh))


def solve_kernel(pos, mine, other, b_ref, xh, xl, base, mat, ah, al, own, sem):
    y, core = pos[0], pos[1]

    def place(src, c):
        @pl.loop(0, NY)
        def _(d):
            r = pl.multiple_of((y + d) % NY * 128 + c * PB, PB)
            for s in range(SLOTS):
                for xs in range(NX):
                    mat[s, pl.ds(r, PB), xs * 128 : (xs + 1) * 128] = src[d, s * 4 + xs]

    for c in range(2):

        @pl.when(core == c)
        def _(c=c):
            place(mine, c)

        @pl.when(core != c)
        def _(c=c):
            place(other, c)

    row = lax.broadcasted_iota(jnp.int32, (128, 128), 0) // PB
    col = lax.broadcasted_iota(jnp.int32, (128, 128), 1) // PB
    inv = {}
    for p in range(PANELS):
        for b in range(4):
            blk = mat[p, b * 128 : (b + 1) * 128, b * 128 : (b + 1) * 128]
            diag = jnp.where(row == col, blk, 0.0)
            low = jnp.where(row > col, blk, 0.0)
            inv[p, b] = diag - exact_dot(diag, exact_dot(low, diag))
    for p in range(PANELS):
        for b in range(4):
            mat[p, b * 128 : (b + 1) * 128, b * 128 : (b + 1) * 128] = inv[p, b]
    for size in (128, 256):
        for p in range(PANELS):
            for b in range(0, PANEL // size, 2):
                lo, mid, hi = b * size, (b + 1) * size, (b + 2) * size
                off = exact_dot(
                    mat[p, mid:hi, mid:hi],
                    exact_dot(mat[p, mid:hi, lo:mid], mat[p, lo:mid, lo:mid]),
                )
                mat[p, mid:hi, lo:mid] = -off

    slot_of = {(1, 0): 3, (2, 0): 4, (2, 1): 5}
    for p in range(PANELS):
        rhs = jnp.concatenate(
            [b_ref[r * WIN + p * PB : r * WIN + (p + 1) * PB, :] for r in range(8)], axis=0
        )
        for q in range(p):
            part = slice(q * PANEL, (q + 1) * PANEL)
            rhs = rhs - dot3(*split(mat[slot_of[p, q]]), ah[part, :], al[part, :])
        x = dot3(*split(mat[p]), *split(rhs))
        part = slice(p * PANEL, (p + 1) * PANEL)
        hi, lo = split(x)
        ah[part, :] = hi
        al[part, :] = lo
        for r in range(8):

            @pl.when(y * 2 + core == r)
            def _(r=r, x=x, p=p):
                own[p * PB : (p + 1) * PB, :] = x[r * PB : (r + 1) * PB, :]

        for k, i in enumerate(GROUP_ORDER):
            for j in range(4):
                src = pl.multiple_of(p * PANEL + source(pos, i, j) * CB, CB)
                dst = (k * PANELS + p) * 128 + j * CB
                xh[dst : dst + CB, :] = ah[pl.ds(src, CB), :]
                xl[dst : dst + CB, :] = al[pl.ds(src, CB), :]
    copy = pltpu.make_async_copy(own, base.at[0:WIN, :], sem)
    copy.start()
    copy.wait()


def update_kernel(blocks_of, *refs):
    n = len(blocks_of)
    lrefs, (xh, xl, r_ref), (out, lh, ll) = refs[:n], refs[n : n + 3], refs[-3:]
    g = pl.program_id(0)
    lane = lax.broadcasted_iota(jnp.int32, (GR, 128), 1) // CB
    blocks = [(ref, b) for ref, count in zip(lrefs, blocks_of) for b in range(count)]
    for i in range(len(blocks) // 4):
        for p in range(PANELS):
            total = None
            for j in range(4):
                ref, b = blocks[i * 4 + j]
                v = pltpu.roll(ref[b, p * GR : (p + 1) * GR, :], (j - g) % 4 * CB, 1)
                total = v if total is None else jnp.where(lane == j, v, total)
            k = (i * PANELS + p) * 128
            hi, lo = split(total)
            lh[:, k : k + 128] = hi
            ll[:, k : k + 128] = lo
    for c in range(0, NCOL, 256):
        w = slice(c, min(c + 256, NCOL))
        out[:, w] = r_ref[:, w] - dot3(lh[...], ll[...], xh[:, w], xl[:, w])


VM = pl.BlockSpec(memory_space=pltpu.VMEM)
SM = pl.BlockSpec(memory_space=pltpu.SMEM)
ANY = pl.BlockSpec(memory_space=pl.ANY)


def params(limit):
    return pltpu.CompilerParams(vmem_limit_bytes=limit * MIB)


def cost(flops, moved):
    return pl.CostEstimate(flops=int(flops), bytes_accessed=int(moved), transcendentals=0)


def update(carried, lparts, xh, xl, kblock):
    depth = sum(v.shape[0] for v in lparts) // 4 * PANELS * 128
    strip = pl.BlockSpec(
        (pl.Element(GR), pl.Element(NCOL)), lambda g: (pl.multiple_of(WIN + g * GR, 16), 0)
    )
    n = len(lparts)
    return pl.pallas_call(
        lambda *refs: update_kernel([v.shape[0] for v in lparts], *refs),
        grid=(GROUPS,),
        out_shape=jax.ShapeDtypeStruct((ROWS, NCOL), F32),
        in_specs=[pl.BlockSpec(v.shape, lambda g: (0, 0, 0)) for v in lparts]
        + [pl.BlockSpec((depth, NCOL), lambda g: (kblock, 0))] * 2
        + [strip, ANY][: len(carried)],
        out_specs=strip,
        scratch_shapes=[pltpu.VMEM((GR, depth), BF16)] * 2,
        input_output_aliases={n + 1 + len(carried): 0},
        compiler_params=params(56),
        cost_estimate=cost(6 * TRAIL * depth * NCOL, 30e6),
    )(*lparts, xh, xl, *carried)


def local(rhs_tile, factor):
    row_i, col_i = lax.axis_index("row"), lax.axis_index("col")
    pos = jnp.stack([row_i // 2, row_i % 2, col_i // NZ, col_i % NZ]).astype(jnp.int32)

    window = lax.all_gather(rhs_tile[:WIN], "row", axis=0, tiled=True)

    packed, w = pl.pallas_call(
        pack_kernel,
        out_shape=(
            jax.ShapeDtypeStruct((PANELS * GR, 128), F32),
            jax.ShapeDtypeStruct((2 * PB, 128), F32),
        ),
        in_specs=[VM],
        out_specs=(VM, VM),
        compiler_params=params(8),
    )(factor)

    w1 = jnp.stack([w] + [from_first(w, d) for d in (1, 2, 3)])
    groups = [w1] + [from_second(w1, d) for d in (1, 2, 3)]

    mine = pl.pallas_call(
        rows_kernel,
        out_shape=jax.ShapeDtypeStruct((SLOTS * 4, PB, 128), F32),
        in_specs=[SM] + [VM] * 4,
        out_specs=VM,
        scratch_shapes=[pltpu.VMEM((16, 2 * PB, 128), F32)],
        compiler_params=params(8),
    )(pos, *groups)

    u1, u3 = from_first(packed, 1), from_first(packed, 3)
    h = PANELS * GR // 2
    u2 = jnp.concatenate([from_first(u1[:h], 1), from_first(u3[h:], 3)])
    q0 = jnp.stack([packed, u1, u2, u3])
    q1, q3 = from_second(q0, 1), from_second(q0, 3)
    q2 = (from_second(q1[:2], 1), from_second(q3[2:], 3))

    m1, m3 = from_y(mine, 1), from_y(mine, 3)
    hs = SLOTS * 2
    m2 = jnp.concatenate([from_y(m1[:hs], 1), from_y(m3[hs:], 3)])
    chip = jnp.stack([mine, m1, m2, m3])
    other = from_core(chip)

    xh, xl, base = pl.pallas_call(
        solve_kernel,
        out_shape=(
            jax.ShapeDtypeStruct((PANELS * PANEL, NCOL), BF16),
            jax.ShapeDtypeStruct((PANELS * PANEL, NCOL), BF16),
            jax.ShapeDtypeStruct((ROWS, NCOL), F32),
        ),
        in_specs=[SM, VM, VM, VM],
        out_specs=(VM, VM, ANY),
        scratch_shapes=[
            pltpu.VMEM((SLOTS, PANEL, PANEL), F32),
            pltpu.VMEM((PANELS * PANEL, NCOL), BF16),
            pltpu.VMEM((PANELS * PANEL, NCOL), BF16),
            pltpu.VMEM((WIN, NCOL), F32),
            pltpu.SemaphoreType.DMA,
        ],
        compiler_params=params(56),
        cost_estimate=cost(36 * PANEL * PANEL * NCOL, 20e6),
    )(pos, chip, other, window)

    base = update((rhs_tile, base), [q0, q1, q3], xh, xl, 0)
    return update((base,), list(q2), xh, xl, 3)


def solution(mesh):
    spec = P("row", "col")
    return jax.shard_map(
        local, mesh=mesh, in_specs=(spec, spec), out_specs=spec, check_vma=False
    )
```

```python
import jax
import jax.numpy as jnp
from jax import lax
from jax.experimental import pallas as pl
from jax.experimental.pallas import tpu as pltpu
from jax.sharding import PartitionSpec as P

F32, BF16 = jnp.float32, jnp.bfloat16
NX, NY, NZ = 4, 4, 4
ROWS, NCOL = 2304, 1152
PB, CB, PANEL, PANELS = 64, 32, 512, 3
WIN = PB * PANELS
TRAIL = ROWS - WIN
GROUPS = 4
GR = TRAIL // GROUPS
SLOTS = 6
MIB = 1024 * 1024
GROUP_ORDER = (0, 1, 3, 2)


def joint(v, dest):
    pairs = []
    for y in range(NY):
        for c in range(2):
            for x in range(NX):
                for z in range(NZ):
                    ty, tc, tx, tz = dest(y, c, x, z)
                    pairs.append(
                        (
                            (y * 2 + c) * 16 + x * 4 + z,
                            ((ty % NY) * 2 + tc % 2) * 16 + (tx % NX) * 4 + tz % NZ,
                        )
                    )
    return lax.ppermute(v, ("row", "col"), pairs)


def from_first(v, d):
    return joint(v, lambda y, c, x, z: (y, c, x - d, z) if c == 0 else (y, c, x, z - d))


def from_second(v, d):
    return joint(v, lambda y, c, x, z: (y, c, x, z - d) if c == 0 else (y, c, x - d, z))


def from_y(v, d):
    return joint(v, lambda y, c, x, z: (y - d, c, x, z))


def from_core(v):
    return joint(v, lambda y, c, x, z: (y, 1 - c, x, z))


def pack_kernel(f_ref, r_ref, l_ref, w_ref, b_ref, sem):
    copy = pltpu.make_async_copy(r_ref.at[0:WIN, :], b_ref, sem)
    copy.start()
    for p in range(PANELS):
        l_ref[p * GR : (p + 1) * GR, :] = jnp.concatenate(
            [
                f_ref[WIN + g * GR : WIN + (g + 1) * GR, p * CB : (p + 1) * CB]
                for g in range(GROUPS)
            ],
            axis=1,
        )

    def block(i, j):
        return f_ref[i * PB : (i + 1) * PB, j * CB : (j + 1) * CB]

    w_ref[0:PB, :] = jnp.concatenate([block(0, 0), block(1, 1), block(2, 2), block(1, 0)], axis=1)
    zero = jnp.zeros((PB, CB), F32)
    w_ref[PB : 2 * PB, :] = jnp.concatenate([block(2, 0), block(2, 1), zero, zero], axis=1)
    copy.wait()


def source(pos, i, j):
    core, x, z = pos[1], pos[2], pos[3]
    xs = jnp.where(core == 0, x + j, x + i) % NX
    zs = jnp.where(core == 0, z + i, z + j) % NZ
    return xs * NZ + zs


def rows_kernel(pos, g0, g1, g2, g3, out, canon, diag):
    y, core = pos[0], pos[1]
    for i, ref in enumerate((g0, g1, g2, g3)):
        for j in range(4):
            canon[source(pos, i, j)] = ref[j]
    lane = lax.broadcasted_iota(jnp.int32, (PB, 128), 1)
    row = lax.broadcasted_iota(jnp.int32, (PB, 128), 0)
    for s in range(SLOTS):
        half, q = divmod(s, 4)
        for xs in range(NX):
            total = None
            for zs in range(NZ):
                v = canon[xs * NZ + zs, half * PB : (half + 1) * PB, :]
                shift = (zs - q) % 4 * CB
                v = pltpu.roll(v, shift, 1) if shift else v
                total = v if total is None else jnp.where(lane // CB == zs, v, total)
            out[s, :, xs * 128 : (xs + 1) * 128] = total
            if s < PANELS:
                diag[s, xs] = total
    eye = (lane == row).astype(F32)
    blocks, mats, sols = [], [], []
    for p in range(PANELS):
        blk = diag[p, y]
        blocks.append(blk)
        a = jnp.where(core == 1, pltpu.roll(blk, PB, 1), blk)
        mats.append((a, a - eye))
        sols.append([eye[8 * k : 8 * k + 8] for k in range(PB // 8)])
    for i in range(PB):
        for p in range(PANELS):
            a, am = mats[p]
            k0, r0 = divmod(i, 8)
            top = sols[p][k0][r0 : r0 + 1, :] * (1.0 / a[i : i + 1, i : i + 1])
            for k in range(k0, PB // 8):
                sols[p][k] = sols[p][k] - am[8 * k : 8 * k + 8, i : i + 1] * top
    for p in range(PANELS):
        inv = jnp.concatenate(sols[p], axis=0)
        inv = jnp.where(core == 1, pltpu.roll(inv, PB, 1), inv)
        inv = jnp.where(lane // PB == core, inv, blocks[p])
        for k in range(NY):

            @pl.when(y == k)
            def _(p=p, k=k, inv=inv):
                out[p, :, k * 128 : (k + 1) * 128] = inv


def exact_dot(a, b):
    return jnp.dot(a, b, precision=lax.Precision.HIGHEST, preferred_element_type=F32)


def split(v):
    hi = v.astype(BF16)
    return hi, (v - hi.astype(F32)).astype(BF16)


def dot3(a, b):
    return jnp.dot(
        jnp.concatenate([a[0], a[0], a[1]], axis=1),
        jnp.concatenate([b[0], b[1], b[0]], axis=0),
        preferred_element_type=F32,
    )


COLS = [slice(c, min(c + 256, NCOL)) for c in range(0, NCOL, 256)]


def solve_kernel(
    pos, mine, other, bmine, bother, xh, xl, base, mat, b_ref, lh, ll, oh, ol, rh, rl, ah, al, xs, own, sem, last
):
    y, core = pos[0], pos[1]

    def copies(to, sources, sems):
        made = []
        for which, src in enumerate(sources):
            c = core if which == 0 else 1 - core
            for d in range(NY):
                r = pl.multiple_of((y + d) % NY * 128 + c * PB, PB)
                made.append(
                    pltpu.make_async_copy(
                        src.at[d], to.at[:, pl.ds(r, PB), :], sems.at[which * NY + d]
                    )
                )
        return made

    mat_copies = copies(mat, (mine, other), sem.at[0])
    b_copies = copies(b_ref, (bmine, bother), sem.at[1])
    for copy in mat_copies + b_copies:
        copy.start()
    for copy in mat_copies:
        copy.wait()

    row = lax.broadcasted_iota(jnp.int32, (128, 128), 0) // PB
    col = lax.broadcasted_iota(jnp.int32, (128, 128), 1) // PB
    inv = {}
    for p in range(PANELS):
        for b in range(4):
            blk = mat[p, b * 128 : (b + 1) * 128, b * 128 : (b + 1) * 128]
            diag = jnp.where(row == col, blk, 0.0)
            low = jnp.where(row > col, blk, 0.0)
            inv[p, b] = diag - exact_dot(diag, exact_dot(low, diag))
    for p in range(PANELS):
        for b in range(4):
            mat[p, b * 128 : (b + 1) * 128, b * 128 : (b + 1) * 128] = inv[p, b]
    for size in (128, 256):
        for p in range(PANELS):
            for b in range(0, PANEL // size, 2):
                lo, mid, hi = b * size, (b + 1) * size, (b + 2) * size
                off = exact_dot(
                    mat[p, mid:hi, mid:hi],
                    exact_dot(mat[p, mid:hi, lo:mid], mat[p, lo:mid, lo:mid]),
                )
                mat[p, mid:hi, lo:mid] = -off
    for p in range(PANELS):
        lh[p], ll[p] = split(mat[p])
        oh[p], ol[p] = split(mat[PANELS + p])

    for copy in b_copies:
        copy.wait()
    left = {1: (0,), 2: (1, 2)}
    half = PANEL // 2
    for p in range(PANELS):
        for w in COLS:
            rhs = b_ref[p, :, w]
            if p:
                o = [jnp.concatenate([v[k] for k in left[p]], axis=1) for v in (oh, ol)]
                rhs = rhs - dot3(o, [v[: p * PANEL, w] for v in (ah, al)])
            rh[p, :, w], rl[p, :, w] = split(rhs)
        for w in COLS:
            for top, depth in ((0, half), (half, PANEL)):
                x = dot3(
                    [v[p, top : top + half, :depth] for v in (lh, ll)],
                    [v[p, :depth, w] for v in (rh, rl)],
                )
                part = slice(p * PANEL + top, p * PANEL + top + half)
                xs[top : top + half, w] = x
                ah[part, w], al[part, w] = split(x)
        mine_rows = pl.multiple_of((y * 2 + core) * PB, PB)
        own[p * PB : (p + 1) * PB, :] = xs[pl.ds(mine_rows, PB), :]
        for k, i in enumerate(GROUP_ORDER):
            for j in range(4):
                src = pl.multiple_of(p * PANEL + source(pos, i, j) * CB, CB)
                dst = (k * PANELS + p) * 128 + j * CB
                xh[dst : dst + CB, :] = ah[pl.ds(src, CB), :]
                xl[dst : dst + CB, :] = al[pl.ds(src, CB), :]
    copy = pltpu.make_async_copy(own, base.at[0:WIN, :], last)
    copy.start()
    copy.wait()


def assemble_kernel(*refs):
    lrefs, (lh, ll) = refs[:-2], refs[-2:]
    g = pl.program_id(0)
    lane = lax.broadcasted_iota(jnp.int32, (GR, 128), 1) // CB
    blocks = [(ref, b) for ref in lrefs for b in range(ref.shape[0])]
    for p in range(PANELS):
        total = None
        for j, (ref, b) in enumerate(blocks):
            v = pltpu.roll(ref[b, p * GR : (p + 1) * GR, :], (j - g) % 4 * CB, 1)
            total = v if total is None else jnp.where(lane == j, v, total)
        k = p * 128
        lh[:, k : k + 128], ll[:, k : k + 128] = split(total)


def update_kernel(*refs):
    his, los, (xh, xl, r_ref, _base, out) = refs[:4], refs[4:8], refs[8:]
    a = [jnp.concatenate([v[...] for v in part], axis=1) for part in (his, los)]
    for w in COLS:
        out[:, w] = r_ref[:, w] - dot3(a, (xh[:, w], xl[:, w]))


VM = pl.BlockSpec(memory_space=pltpu.VMEM)
SM = pl.BlockSpec(memory_space=pltpu.SMEM)
ANY = pl.BlockSpec(memory_space=pl.ANY)
SUB = PANELS * 128
DEPTH = PANELS * PANEL


def params(limit):
    return pltpu.CompilerParams(vmem_limit_bytes=limit * MIB)


def cost(flops, moved):
    return pl.CostEstimate(flops=int(flops), bytes_accessed=int(moved), transcendentals=0)


def assemble(*blocks):
    out = jax.ShapeDtypeStruct((GROUPS, GR, SUB), BF16)
    spec = pl.BlockSpec((None, GR, SUB), lambda g: (g, 0, 0))
    return pl.pallas_call(
        assemble_kernel,
        grid=(GROUPS,),
        out_shape=(out, out),
        in_specs=[pl.BlockSpec(v.shape, lambda g: (0, 0, 0)) for v in blocks],
        out_specs=(spec, spec),
        compiler_params=params(20),
        cost_estimate=cost(4e6, 7e6),
    )(*blocks)


def update(rows_in, base, parts, xh, xl):
    strip = pl.BlockSpec(
        (pl.Element(GR), pl.Element(NCOL)), lambda g: (pl.multiple_of(WIN + g * GR, 16), 0)
    )
    spec = pl.BlockSpec((None, GR, SUB), lambda g: (g, 0, 0))
    whole = pl.BlockSpec((DEPTH, NCOL), lambda g: (0, 0))
    return pl.pallas_call(
        update_kernel,
        grid=(GROUPS,),
        out_shape=jax.ShapeDtypeStruct((ROWS, NCOL), F32),
        in_specs=[spec] * 8 + [whole, whole, strip, ANY],
        out_specs=strip,
        input_output_aliases={11: 0},
        compiler_params=params(48),
        cost_estimate=cost(6 * TRAIL * DEPTH * NCOL, 30e6),
    )(*[v[0] for v in parts], *[v[1] for v in parts], xh, xl, rows_in, base)


def local(rhs_tile, factor):
    row_i, col_i = lax.axis_index("row"), lax.axis_index("col")
    pos = jnp.stack([row_i // 2, row_i % 2, col_i // NZ, col_i % NZ]).astype(jnp.int32)

    packed, w, b0 = pl.pallas_call(
        pack_kernel,
        out_shape=(
            jax.ShapeDtypeStruct((PANELS * GR, 128), F32),
            jax.ShapeDtypeStruct((2 * PB, 128), F32),
            jax.ShapeDtypeStruct((WIN, NCOL), F32),
        ),
        in_specs=[VM, ANY],
        out_specs=(VM, VM, VM),
        scratch_shapes=[pltpu.SemaphoreType.DMA],
        compiler_params=params(57),
    )(factor, rhs_tile)

    w1 = jnp.stack([w] + [from_first(w, d) for d in (1, 2, 3)])
    groups = [w1] + [from_second(w1, d) for d in (1, 2, 3)]

    mine = pl.pallas_call(
        rows_kernel,
        out_shape=jax.ShapeDtypeStruct((SLOTS, PB, PANEL), F32),
        in_specs=[SM] + [VM] * 4,
        out_specs=VM,
        scratch_shapes=[
            pltpu.VMEM((16, 2 * PB, 128), F32),
            pltpu.VMEM((PANELS, NX, PB, 128), F32),
        ],
        compiler_params=params(8),
    )(pos, *groups)

    b1, b3 = from_y(b0, 1), from_y(b0, 3)
    hb = WIN // 2
    b2 = jnp.concatenate([from_y(b1[:hb], 1), from_y(b3[hb:], 3)])
    bchip = jnp.stack([b0, b1, b2, b3]).reshape(NY, PANELS, PB, NCOL)
    bother = from_core(bchip)

    u1, u3 = from_first(packed, 1), from_first(packed, 3)
    h = PANELS * GR // 2
    u2 = jnp.concatenate([from_first(u1[:h], 1), from_first(u3[h:], 3)])
    q0 = jnp.stack([packed, u1, u2, u3])
    q1, q3 = from_second(q0, 1), from_second(q0, 3)
    q2 = (from_second(q1[:2], 1), from_second(q3[2:], 3))

    m1, m3 = from_y(mine, 1), from_y(mine, 3)
    m1, m3, _ = lax.optimization_barrier((m1, m3, q0[0, 0, 0]))
    hs = SLOTS // 2
    m2 = jnp.concatenate([from_y(m1[:hs], 1), from_y(m3[hs:], 3)])
    chip = jnp.stack([mine, m1, m2, m3])
    other = from_core(chip)

    parts = [assemble(q0), assemble(q1), assemble(q3)]
    pos_late, _, _ = lax.optimization_barrier((pos, q1[0, 0, 0], q3[0, 0, 0]))
    xh, xl, base = pl.pallas_call(
        solve_kernel,
        out_shape=(
            jax.ShapeDtypeStruct((DEPTH, NCOL), BF16),
            jax.ShapeDtypeStruct((DEPTH, NCOL), BF16),
            jax.ShapeDtypeStruct((ROWS, NCOL), F32),
        ),
        in_specs=[SM, ANY, ANY, ANY, ANY],
        out_specs=(VM, VM, ANY),
        scratch_shapes=[
            pltpu.VMEM((SLOTS, PANEL, PANEL), F32),
            pltpu.VMEM((PANELS, PANEL, NCOL), F32),
        ]
        + [pltpu.VMEM((PANELS, PANEL, PANEL), BF16)] * 4
        + [pltpu.VMEM((PANELS, PANEL, NCOL), BF16)] * 2
        + [pltpu.VMEM((DEPTH, NCOL), BF16)] * 2
        + [
            pltpu.VMEM((PANEL, NCOL), F32),
            pltpu.VMEM((WIN, NCOL), F32),
            pltpu.SemaphoreType.DMA((2, 2 * NY)),
            pltpu.SemaphoreType.DMA,
        ],
        compiler_params=params(48),
        cost_estimate=cost(36 * PANEL * PANEL * NCOL, 20e6),
    )(pos_late, chip, other, bchip, bother)

    return update(rhs_tile, base, parts + [assemble(*q2)], xh, xl)


def solution(mesh):
    spec = P("row", "col")
    return jax.shard_map(
        local, mesh=mesh, in_specs=(spec, spec), out_specs=spec, check_vma=False
    )
```

```python
import jax
import jax.numpy as jnp
from jax import lax
from jax.experimental import pallas as pl
from jax.experimental.pallas import tpu as pltpu
from jax.sharding import PartitionSpec as P

F32, BF16 = jnp.float32, jnp.bfloat16
NX, NY, NZ = 4, 4, 4
ROWS, NCOL = 2304, 1152
PB, CB, PANEL, PANELS = 64, 32, 512, 3
WIN = PB * PANELS
TRAIL = ROWS - WIN
GROUPS = 4
GR = TRAIL // GROUPS
SLOTS = 6
WR = 2 * PB
MIB = 1024 * 1024
GROUP_ORDER = (0, 1, 3, 2)


def joint(v, dest):
    pairs = []
    for y in range(NY):
        for c in range(2):
            for x in range(NX):
                for z in range(NZ):
                    ty, tc, tx, tz = dest(y, c, x, z)
                    pairs.append(
                        (
                            (y * 2 + c) * 16 + x * 4 + z,
                            ((ty % NY) * 2 + tc % 2) * 16 + (tx % NX) * 4 + tz % NZ,
                        )
                    )
    return lax.ppermute(v, ("row", "col"), pairs)


def from_first(v, d):
    return joint(v, lambda y, c, x, z: (y, c, x - d, z) if c == 0 else (y, c, x, z - d))


def from_second(v, d):
    return joint(v, lambda y, c, x, z: (y, c, x, z - d) if c == 0 else (y, c, x - d, z))


def along_y(v):
    return joint(v, lambda y, c, x, z: (y - 1 if c == 0 else y + 1, c, x, z))


def from_core(v):
    return joint(v, lambda y, c, x, z: (y, 1 - c, x, z))


def pack_kernel(f_ref, l_ref):
    for p in range(PANELS):
        l_ref[WR + p * GR : WR + (p + 1) * GR, :] = jnp.concatenate(
            [
                f_ref[WIN + g * GR : WIN + (g + 1) * GR, p * CB : (p + 1) * CB]
                for g in range(GROUPS)
            ],
            axis=1,
        )

    def block(i, j):
        return f_ref[i * PB : (i + 1) * PB, j * CB : (j + 1) * CB]

    l_ref[0:PB, :] = jnp.concatenate([block(0, 0), block(1, 1), block(2, 2), block(1, 0)], axis=1)
    zero = jnp.zeros((PB, CB), F32)
    l_ref[PB:WR, :] = jnp.concatenate([block(2, 0), block(2, 1), zero, zero], axis=1)


def source(pos, i, j):
    core, x, z = pos[1], pos[2], pos[3]
    xs = jnp.where(core == 0, x + j, x + i) % NX
    zs = jnp.where(core == 0, z + i, z + j) % NZ
    return xs * NZ + zs


def rows_kernel(pos, g0, g1, g2, g3, _after, out, canon, diag):
    y, core = pos[0], pos[1]
    for i, ref in enumerate((g0, g1, g2, g3)):
        for j in range(4):
            canon[source(pos, i, j)] = ref[j]
    lane = lax.broadcasted_iota(jnp.int32, (PB, 128), 1)
    row = lax.broadcasted_iota(jnp.int32, (PB, 128), 0)
    for s in range(SLOTS):
        half, q = divmod(s, 4)
        for xs in range(NX):
            total = None
            for zs in range(NZ):
                v = canon[xs * NZ + zs, half * PB : (half + 1) * PB, :]
                shift = (zs - q) % 4 * CB
                v = pltpu.roll(v, shift, 1) if shift else v
                total = v if total is None else jnp.where(lane // CB == zs, v, total)
            out[s, :, xs * 128 : (xs + 1) * 128] = total
            if s < PANELS:
                diag[s, xs] = total
    eye = (lane == row).astype(F32)
    blocks, mats, sols = [], [], []
    for p in range(PANELS):
        blk = diag[p, y]
        blocks.append(blk)
        a = jnp.where(core == 1, pltpu.roll(blk, PB, 1), blk)
        mats.append((a, a - eye))
        sols.append([eye[8 * k : 8 * k + 8] for k in range(PB // 8)])
    for i in range(PB):
        for p in range(PANELS):
            a, am = mats[p]
            k0, r0 = divmod(i, 8)
            top = sols[p][k0][r0 : r0 + 1, :] * (1.0 / a[i : i + 1, i : i + 1])
            for k in range(k0, PB // 8):
                sols[p][k] = sols[p][k] - am[8 * k : 8 * k + 8, i : i + 1] * top
    for p in range(PANELS):
        inv = jnp.concatenate(sols[p], axis=0)
        inv = jnp.where(core == 1, pltpu.roll(inv, PB, 1), inv)
        inv = jnp.where(lane // PB == core, inv, blocks[p])
        for k in range(NY):

            @pl.when(y == k)
            def _(p=p, k=k, inv=inv):
                out[p, :, k * 128 : (k + 1) * 128] = inv


def exact_dot(a, b):
    return jnp.dot(a, b, precision=lax.Precision.HIGHEST, preferred_element_type=F32)


def split(v):
    hi = v.astype(BF16)
    return hi, (v - hi.astype(F32)).astype(BF16)


def dot3(a, b):
    return jnp.dot(
        jnp.concatenate([a[0], a[0], a[1]], axis=1),
        jnp.concatenate([b[0], b[1], b[0]], axis=0),
        preferred_element_type=F32,
    )


COLS = [slice(c, min(c + 256, NCOL)) for c in range(0, NCOL, 256)]


def solve_kernel(
    pos, m0, mc, mown, mgot, b0, bc, bown, bgot, xh, xl, base, mat, b_ref, lh, ll, oh, ol, rh, rl, ah, al, xs, own, sem, last
):
    y, core = pos[0], pos[1]

    near, far = 1 + 2 * core, 3 - 2 * core

    def copies(to, own_rows, pair_rows, own3, got3, sems):
        made = []
        plan = (
            (own_rows, 0, core),
            (pair_rows, 0, 1 - core),
            (own3.at[0], near, core),
            (own3.at[1], near, 1 - core),
            (own3.at[2], 2, core),
            (got3.at[0], far, 1 - core),
            (got3.at[1], far, core),
            (got3.at[2], 2, 1 - core),
        )
        for k, (src, d, c) in enumerate(plan):
            r = pl.multiple_of((y + d) % NY * 128 + c * PB, PB)
            made.append(pltpu.make_async_copy(src, to.at[:, pl.ds(r, PB), :], sems.at[k]))
        return made

    mat_copies = copies(mat, m0, mc, mown, mgot, sem.at[0])
    b_copies = copies(b_ref, b0, bc, bown, bgot, sem.at[1])
    for copy in mat_copies + b_copies:
        copy.start()
    for copy in mat_copies:
        copy.wait()

    row = lax.broadcasted_iota(jnp.int32, (128, 128), 0) // PB
    col = lax.broadcasted_iota(jnp.int32, (128, 128), 1) // PB
    inv = {}
    for p in range(PANELS):
        for b in range(4):
            blk = mat[p, b * 128 : (b + 1) * 128, b * 128 : (b + 1) * 128]
            diag = jnp.where(row == col, blk, 0.0)
            low = jnp.where(row > col, blk, 0.0)
            inv[p, b] = diag - exact_dot(diag, exact_dot(low, diag))
    for p in range(PANELS):
        for b in range(4):
            mat[p, b * 128 : (b + 1) * 128, b * 128 : (b + 1) * 128] = inv[p, b]
    for size in (128, 256):
        for p in range(PANELS):
            for b in range(0, PANEL // size, 2):
                lo, mid, hi = b * size, (b + 1) * size, (b + 2) * size
                off = exact_dot(
                    mat[p, mid:hi, mid:hi],
                    exact_dot(mat[p, mid:hi, lo:mid], mat[p, lo:mid, lo:mid]),
                )
                mat[p, mid:hi, lo:mid] = -off
    for p in range(PANELS):
        lh[p], ll[p] = split(mat[p])
        oh[p], ol[p] = split(mat[PANELS + p])

    for copy in b_copies:
        copy.wait()
    left = {1: (0,), 2: (1, 2)}
    half = PANEL // 2
    for p in range(PANELS):
        for w in COLS:
            rhs = b_ref[p, :, w]
            if p:
                o = [jnp.concatenate([v[k] for k in left[p]], axis=1) for v in (oh, ol)]
                rhs = rhs - dot3(o, [v[: p * PANEL, w] for v in (ah, al)])
            rh[:, w], rl[:, w] = split(rhs)
        for w in COLS:
            for top, depth in ((0, half), (half, PANEL)):
                x = dot3(
                    [v[p, top : top + half, :depth] for v in (lh, ll)],
                    [v[:depth, w] for v in (rh, rl)],
                )
                part = slice(p * PANEL + top, p * PANEL + top + half)
                xs[top : top + half, w] = x
                ah[part, w], al[part, w] = split(x)
        mine_rows = pl.multiple_of((y * 2 + core) * PB, PB)
        own[p * PB : (p + 1) * PB, :] = xs[pl.ds(mine_rows, PB), :]
        for k, i in enumerate(GROUP_ORDER):
            for j in range(4):
                src = pl.multiple_of(p * PANEL + source(pos, i, j) * CB, CB)
                dst = (k * PANELS + p) * 128 + j * CB
                xh[dst : dst + CB, :] = ah[pl.ds(src, CB), :]
                xl[dst : dst + CB, :] = al[pl.ds(src, CB), :]
    copy = pltpu.make_async_copy(own, base.at[0:WIN, :], last)
    copy.start()
    copy.wait()


def lanes_in_order(lrefs, lh, ll):
    g = pl.program_id(0)
    lane = lax.broadcasted_iota(jnp.int32, (GR, 128), 1) // CB
    blocks = [(ref, b) for ref in lrefs for b in range(ref.shape[0])]
    for p in range(PANELS):
        total = None
        for j, (ref, b) in enumerate(blocks):
            v = pltpu.roll(ref[b, p * GR : (p + 1) * GR, :], (j - g) % 4 * CB, 1)
            total = v if total is None else jnp.where(lane == j, v, total)
        k = p * 128
        lh[:, k : k + 128], ll[:, k : k + 128] = split(total)


def assemble_kernel(*refs):
    lanes_in_order(refs[:-2], *refs[-2:])


def update_kernel(*refs):
    his, los, (qa, qb, xh, xl, r_ref, _base, out, lh, ll) = refs[:3], refs[3:6], refs[6:]
    lanes_in_order((qa, qb), lh, ll)
    a = [
        jnp.concatenate([v[...] for v in (*part, last)], axis=1)
        for part, last in ((his, lh), (los, ll))
    ]
    for w in COLS:
        out[:, w] = r_ref[:, w] - dot3(a, (xh[:, w], xl[:, w]))


VM = pl.BlockSpec(memory_space=pltpu.VMEM)
SM = pl.BlockSpec(memory_space=pltpu.SMEM)
ANY = pl.BlockSpec(memory_space=pl.ANY)
SUB = PANELS * 128
DEPTH = PANELS * PANEL


def params(limit):
    return pltpu.CompilerParams(vmem_limit_bytes=limit * MIB)


def cost(flops, moved):
    return pl.CostEstimate(flops=int(flops), bytes_accessed=int(moved), transcendentals=0)


def assemble(*blocks):
    out = jax.ShapeDtypeStruct((GROUPS, GR, SUB), BF16)
    spec = pl.BlockSpec((None, GR, SUB), lambda g: (g, 0, 0))
    return pl.pallas_call(
        assemble_kernel,
        grid=(GROUPS,),
        out_shape=(out, out),
        in_specs=[pl.BlockSpec(v.shape, lambda g: (0, 0, 0)) for v in blocks],
        out_specs=(spec, spec),
        compiler_params=params(20),
        cost_estimate=cost(4e6, 7e6),
    )(*blocks)


def update(rows_in, base, parts, last, xh, xl):
    strip = pl.BlockSpec(
        (pl.Element(GR), pl.Element(NCOL)), lambda g: (pl.multiple_of(WIN + g * GR, 16), 0)
    )
    spec = pl.BlockSpec((None, GR, SUB), lambda g: (g, 0, 0))
    return pl.pallas_call(
        update_kernel,
        grid=(GROUPS,),
        out_shape=jax.ShapeDtypeStruct((ROWS, NCOL), F32),
        in_specs=[spec] * 6 + [VM] * 4 + [strip, ANY],
        out_specs=strip,
        scratch_shapes=[pltpu.VMEM((GR, SUB), BF16)] * 2,
        input_output_aliases={11: 0},
        compiler_params=params(57),
        cost_estimate=cost(6 * TRAIL * DEPTH * NCOL, 30e6),
    )(*[v[0] for v in parts], *[v[1] for v in parts], *last, xh, xl, rows_in, base)


def moved(arrays, shapes, plan, limit):
    def kernel(*refs):
        sems = refs[-1]
        outs = refs[len(arrays) : -1]
        copies = []
        for k, (i, take, o, put) in enumerate(plan):
            src = refs[i] if take is None else refs[i].at[take]
            dst = outs[o] if put is None else outs[o].at[put]
            copies.append(pltpu.make_async_copy(src, dst, sems.at[k]))
        for copy in copies:
            copy.start()
        for copy in copies:
            copy.wait()

    return pl.pallas_call(
        kernel,
        out_shape=[jax.ShapeDtypeStruct(v, F32) for v in shapes],
        in_specs=[ANY] * len(arrays),
        out_specs=[ANY] * len(shapes),
        scratch_shapes=[pltpu.SemaphoreType.DMA((len(plan),))],
        compiler_params=params(limit),
    )(*arrays)


def second_hop(hop, *after):
    (kept,) = moved(
        (hop, along_y(hop[:1]), *after),
        [(3, *hop.shape[1:])],
        [(0, None, 0, pl.ds(0, 2)), (1, None, 0, pl.ds(2, 1))],
        30,
    )
    return kept, from_core(kept)


def local(rhs_tile, factor):
    row_i, col_i = lax.axis_index("row"), lax.axis_index("col")
    pos = jnp.stack([row_i // 2, row_i % 2, col_i // NZ, col_i % NZ]).astype(jnp.int32)

    packed = pl.pallas_call(
        pack_kernel,
        out_shape=jax.ShapeDtypeStruct((WR + PANELS * GR, 128), F32),
        in_specs=[VM],
        out_specs=VM,
        compiler_params=params(8),
    )(factor)
    rows3 = (PANELS, PB, NCOL)
    (b0,) = moved(
        (rhs_tile,),
        [rows3],
        [(0, pl.ds(p * PB, PB), 0, p) for p in range(PANELS)],
        55,
    )
    bc = from_core(b0)

    u1, u3 = from_first(packed, 1), from_first(packed, 3)
    total = WR + PANELS * GR
    h = WR + PANELS * GR // 2
    f1, f3, bpair = moved(
        (u1, u3, b0, bc),
        [(h, 128), (total - h, 128), (2, *rows3)],
        [(0, pl.ds(0, h), 0, None), (1, pl.ds(h, total - h), 1, None), (2, None, 2, 0), (3, None, 2, 1)],
        57,
    )
    o1, o3 = from_first(f1, 1), from_first(f3, 3)
    bhop = along_y(bpair)

    half = h - WR
    w1, q0 = moved(
        (packed, u1, o1, u3, o3),
        [(4, WR, 128), (4, total - WR, 128)],
        [(j, pl.ds(0, WR), 0, j) for j in range(4)]
        + [(j, pl.ds(WR, total - WR), 1, j) for j in (0, 1, 3)]
        + [
            (2, pl.ds(WR, half), 1, (2, pl.ds(0, half))),
            (4, None, 1, (2, pl.ds(half, half))),
        ],
        57,
    )
    groups = [w1] + [from_second(w1, d) for d in (1, 2, 3)]
    q1, q3 = from_second(q0, 1), from_second(q0, 3)
    q2 = (from_second(q1[:2], 1), from_second(q3[2:], 3))

    mine = pl.pallas_call(
        rows_kernel,
        out_shape=jax.ShapeDtypeStruct((SLOTS, PB, PANEL), F32),
        in_specs=[SM] + [VM] * 4 + [ANY],
        out_specs=VM,
        scratch_shapes=[
            pltpu.VMEM((16, 2 * PB, 128), F32),
            pltpu.VMEM((PANELS, NX, PB, 128), F32),
        ],
        compiler_params=params(8),
    )(pos, *groups, bhop)

    mc = from_core(mine)
    rows = (mine, mc, *second_hop(along_y(jnp.stack([mine, mc])), q1, q3))
    rhs_rows = (b0, bc, *second_hop(bhop))

    parts = [assemble(q0), assemble(q1), assemble(q3)]
    xh, xl, base = pl.pallas_call(
        solve_kernel,
        out_shape=(
            jax.ShapeDtypeStruct((DEPTH, NCOL), BF16),
            jax.ShapeDtypeStruct((DEPTH, NCOL), BF16),
            jax.ShapeDtypeStruct((ROWS, NCOL), F32),
        ),
        in_specs=[SM] + [ANY] * 8,
        out_specs=(VM, VM, ANY),
        scratch_shapes=[
            pltpu.VMEM((SLOTS, PANEL, PANEL), F32),
            pltpu.VMEM((PANELS, PANEL, NCOL), F32),
        ]
        + [pltpu.VMEM((PANELS, PANEL, PANEL), BF16)] * 4
        + [pltpu.VMEM((PANEL, NCOL), BF16)] * 2
        + [pltpu.VMEM((DEPTH, NCOL), BF16)] * 2
        + [
            pltpu.VMEM((PANEL, NCOL), F32),
            pltpu.VMEM((WIN, NCOL), F32),
            pltpu.SemaphoreType.DMA((2, 2 * NY)),
            pltpu.SemaphoreType.DMA,
        ],
        compiler_params=params(45),
        cost_estimate=cost(36 * PANEL * PANEL * NCOL, 20e6),
    )(pos, *rows, *rhs_rows)

    return update(rhs_tile, base, parts, q2, xh, xl)


def solution(mesh):
    spec = P("row", "col")
    return jax.shard_map(
        local, mesh=mesh, in_specs=(spec, spec), out_specs=spec, check_vma=False
    )
```

```python
import jax
import jax.numpy as jnp
from jax import lax
from jax.experimental import pallas as pl
from jax.experimental.pallas import tpu as pltpu
from jax.sharding import PartitionSpec as P

F32, BF16 = jnp.float32, jnp.bfloat16
NX, NY, NZ = 4, 4, 4
ROWS, NCOL = 2304, 1152
PB, CB, PANEL, PANELS = 64, 32, 512, 3
WIN = PB * PANELS
TRAIL = ROWS - WIN
GROUPS = 4
GR = TRAIL // GROUPS
SLOTS = 6
WR = 2 * PB
SUB = PANELS * 128
CHUNK = GR // 3
MIB = 1024 * 1024
GROUP_ORDER = (0, 1, 3, 2)


def joint(v, dest):
    pairs = []
    for y in range(NY):
        for c in range(2):
            for x in range(NX):
                for z in range(NZ):
                    ty, tc, tx, tz = dest(y, c, x, z)
                    pairs.append(
                        (
                            (y * 2 + c) * 16 + x * 4 + z,
                            ((ty % NY) * 2 + tc % 2) * 16 + (tx % NX) * 4 + tz % NZ,
                        )
                    )
    return lax.ppermute(v, ("row", "col"), pairs)


def from_first(v, d):
    return joint(v, lambda y, c, x, z: (y, c, x - d, z) if c == 0 else (y, c, x, z - d))


def from_second(v, d):
    return joint(v, lambda y, c, x, z: (y, c, x, z - d) if c == 0 else (y, c, x - d, z))


def along_y(v):
    return joint(v, lambda y, c, x, z: (y - 1 if c == 0 else y + 1, c, x, z))


def from_core(v):
    return joint(v, lambda y, c, x, z: (y, 1 - c, x, z))


def pack_kernel(f_ref, l_ref):
    for p in range(PANELS):
        l_ref[WR + p * GR : WR + (p + 1) * GR, :] = jnp.concatenate(
            [
                f_ref[WIN + g * GR : WIN + (g + 1) * GR, p * CB : (p + 1) * CB]
                for g in range(GROUPS)
            ],
            axis=1,
        )

    def block(i, j):
        return f_ref[i * PB : (i + 1) * PB, j * CB : (j + 1) * CB]

    l_ref[0:PB, :] = jnp.concatenate([block(0, 0), block(1, 1), block(2, 2), block(1, 0)], axis=1)
    zero = jnp.zeros((PB, CB), F32)
    l_ref[PB:WR, :] = jnp.concatenate([block(2, 0), block(2, 1), zero, zero], axis=1)


def source(pos, i, j):
    core, x, z = pos[1], pos[2], pos[3]
    xs = jnp.where(core == 0, x + j, x + i) % NX
    zs = jnp.where(core == 0, z + i, z + j) % NZ
    return xs * NZ + zs


def rows_kernel(pos, g0, g1, g2, g3, out, canon, diag):
    y, core = pos[0], pos[1]
    for i, ref in enumerate((g0, g1, g2, g3)):
        for j in range(4):
            canon[source(pos, i, j)] = ref[j]
    lane = lax.broadcasted_iota(jnp.int32, (PB, 128), 1)
    row = lax.broadcasted_iota(jnp.int32, (PB, 128), 0)
    for s in range(SLOTS):
        half, q = divmod(s, 4)
        for xs in range(NX):
            total = None
            for zs in range(NZ):
                v = canon[xs * NZ + zs, half * PB : (half + 1) * PB, :]
                shift = (zs - q) % 4 * CB
                v = pltpu.roll(v, shift, 1) if shift else v
                total = v if total is None else jnp.where(lane // CB == zs, v, total)
            out[s, :, xs * 128 : (xs + 1) * 128] = total
            if s < PANELS:
                diag[s, xs] = total
    eye = (lane == row).astype(F32)
    blocks, mats, sols = [], [], []
    for p in range(PANELS):
        blk = diag[p, y]
        blocks.append(blk)
        a = jnp.where(core == 1, pltpu.roll(blk, PB, 1), blk)
        mats.append((a, a - eye))
        sols.append([eye[8 * k : 8 * k + 8] for k in range(PB // 8)])
    for i in range(PB):
        for p in range(PANELS):
            a, am = mats[p]
            k0, r0 = divmod(i, 8)
            top = sols[p][k0][r0 : r0 + 1, :] * (1.0 / a[i : i + 1, i : i + 1])
            for k in range(k0, PB // 8):
                sols[p][k] = sols[p][k] - am[8 * k : 8 * k + 8, i : i + 1] * top
    for p in range(PANELS):
        inv = jnp.concatenate(sols[p], axis=0)
        inv = jnp.where(core == 1, pltpu.roll(inv, PB, 1), inv)
        inv = jnp.where(lane // PB == core, inv, blocks[p])
        for k in range(NY):

            @pl.when(y == k)
            def _(p=p, k=k, inv=inv):
                out[p, :, k * 128 : (k + 1) * 128] = inv


def exact_dot(a, b):
    return jnp.dot(a, b, precision=lax.Precision.HIGHEST, preferred_element_type=F32)


def split(v):
    hi = v.astype(BF16)
    return hi, (v - hi.astype(F32)).astype(BF16)


def dot3(a, b):
    return jnp.dot(
        jnp.concatenate([a[0], a[0], a[1]], axis=1),
        jnp.concatenate([b[0], b[1], b[0]], axis=0),
        preferred_element_type=F32,
    )


COLS = [slice(c, min(c + 256, NCOL)) for c in range(0, NCOL, 256)]


def solve_kernel(
    pos, m0, mc, mown, mgot, b0, bc, bown, bgot, xh, xl, base, mat, b_ref, lh, ll, oh, ol, rh, rl, ah, al, xs, own, sem, last
):
    y, core = pos[0], pos[1]

    near, far = 1 + 2 * core, 3 - 2 * core

    def copies(to, own_rows, pair_rows, own3, got3, sems):
        made = []
        plan = (
            (own_rows, 0, core),
            (pair_rows, 0, 1 - core),
            (own3.at[0], near, core),
            (own3.at[1], near, 1 - core),
            (own3.at[2], 2, core),
            (got3.at[0], far, 1 - core),
            (got3.at[1], far, core),
            (got3.at[2], 2, 1 - core),
        )
        for k, (src, d, c) in enumerate(plan):
            r = pl.multiple_of((y + d) % NY * 128 + c * PB, PB)
            made.append(pltpu.make_async_copy(src, to.at[:, pl.ds(r, PB), :], sems.at[k]))
        return made

    mat_copies = copies(mat, m0, mc, mown, mgot, sem.at[0])
    b_copies = copies(b_ref, b0, bc, bown, bgot, sem.at[1])
    for copy in mat_copies + b_copies:
        copy.start()
    for copy in mat_copies:
        copy.wait()

    row = lax.broadcasted_iota(jnp.int32, (128, 128), 0) // PB
    col = lax.broadcasted_iota(jnp.int32, (128, 128), 1) // PB
    inv = {}
    for p in range(PANELS):
        for b in range(4):
            blk = mat[p, b * 128 : (b + 1) * 128, b * 128 : (b + 1) * 128]
            diag = jnp.where(row == col, blk, 0.0)
            low = jnp.where(row > col, blk, 0.0)
            inv[p, b] = diag - exact_dot(diag, exact_dot(low, diag))
    for p in range(PANELS):
        for b in range(4):
            mat[p, b * 128 : (b + 1) * 128, b * 128 : (b + 1) * 128] = inv[p, b]
    for size in (128, 256):
        for p in range(PANELS):
            for b in range(0, PANEL // size, 2):
                lo, mid, hi = b * size, (b + 1) * size, (b + 2) * size
                off = exact_dot(
                    mat[p, mid:hi, mid:hi],
                    exact_dot(mat[p, mid:hi, lo:mid], mat[p, lo:mid, lo:mid]),
                )
                mat[p, mid:hi, lo:mid] = -off
    for p in range(PANELS):
        lh[p], ll[p] = split(mat[p])
        oh[p], ol[p] = split(mat[PANELS + p])

    for copy in b_copies:
        copy.wait()
    left = {1: (0,), 2: (1, 2)}
    half = PANEL // 2
    for p in range(PANELS):
        for w in COLS:
            rhs = b_ref[p, :, w]
            if p:
                o = [jnp.concatenate([v[k] for k in left[p]], axis=1) for v in (oh, ol)]
                rhs = rhs - dot3(o, [v[: p * PANEL, w] for v in (ah, al)])
            rh[:, w], rl[:, w] = split(rhs)
        for w in COLS:
            for top, depth in ((0, half), (half, PANEL)):
                x = dot3(
                    [v[p, top : top + half, :depth] for v in (lh, ll)],
                    [v[:depth, w] for v in (rh, rl)],
                )
                part = slice(p * PANEL + top, p * PANEL + top + half)
                xs[top : top + half, w] = x
                ah[part, w], al[part, w] = split(x)
        mine_rows = pl.multiple_of((y * 2 + core) * PB, PB)
        own[p * PB : (p + 1) * PB, :] = xs[pl.ds(mine_rows, PB), :]
        for k, i in enumerate(GROUP_ORDER):
            for j in range(4):
                src = pl.multiple_of(p * PANEL + source(pos, i, j) * CB, CB)
                dst = (k * PANELS + p) * 128 + j * CB
                xh[dst : dst + CB, :] = ah[pl.ds(src, CB), :]
                xl[dst : dst + CB, :] = al[pl.ds(src, CB), :]
    copy = pltpu.make_async_copy(own, base.at[0:WIN, :], last)
    copy.start()
    copy.wait()


def lanes_in_order(block, rows, lh, ll):
    lane = lax.broadcasted_iota(jnp.int32, (rows.size, 128), 1)
    low64 = lane < 64
    low32 = lane % 64 < 32
    for p in range(PANELS):
        v = [block(j, p) for j in range(4)]
        for j in range(2):
            a, b = v[j], v[j + 2]
            v[j] = jnp.where(low64, a, pltpu.roll(b, 64, 1))
            v[j + 2] = jnp.where(low64, pltpu.roll(a, 64, 1), b)
        for j in (0, 2):
            a, b = v[j], v[j + 1]
            v[j] = jnp.where(low32, a, pltpu.roll(b, 32, 1))
            v[j + 1] = jnp.where(low32, pltpu.roll(a, 96, 1), b)
        for g in range(GROUPS):
            k = slice(p * 128, (p + 1) * 128)
            lh[g, rows, k], ll[g, rows, k] = split(v[g])


def assemble_kernel(q, lh, ll):
    lanes_in_order(lambda j, p: q[j, p], pl.ds(0, CHUNK), lh, ll)


def update_kernel(*refs):
    his, los, (qa, qb, xh, xl, r_ref, _base, out, lh, ll) = refs[:3], refs[3:6], refs[6:]
    g = pl.program_id(0)

    @pl.when(g == 0)
    def _():
        @pl.loop(0, GR // CHUNK)
        def _(i):
            rows = pl.ds(pl.multiple_of(i * CHUNK, 16), CHUNK)
            lanes_in_order(lambda j, p: (qa, qb)[j // 2][j % 2, p, rows, :], rows, lh, ll)

    a = [
        jnp.concatenate([v[...] for v in part] + [last[g]], axis=1)
        for part, last in ((his, lh), (los, ll))
    ]
    for w in COLS:
        out[:, w] = r_ref[:, w] - dot3(a, (xh[:, w], xl[:, w]))


VM = pl.BlockSpec(memory_space=pltpu.VMEM)
SM = pl.BlockSpec(memory_space=pltpu.SMEM)
ANY = pl.BlockSpec(memory_space=pl.ANY)
DEPTH = PANELS * PANEL


def params(limit):
    return pltpu.CompilerParams(vmem_limit_bytes=limit * MIB)


def cost(flops, moved):
    return pl.CostEstimate(flops=int(flops), bytes_accessed=int(moved), transcendentals=0)


def assemble(q):
    out = jax.ShapeDtypeStruct((GROUPS, GR, SUB), BF16)
    spec = pl.BlockSpec((GROUPS, CHUNK, SUB), lambda i: (0, i, 0))
    return pl.pallas_call(
        assemble_kernel,
        grid=(GR // CHUNK,),
        out_shape=(out, out),
        in_specs=[pl.BlockSpec((4, PANELS, CHUNK, 128), lambda i: (0, 0, i, 0))],
        out_specs=(spec, spec),
        compiler_params=params(12),
        cost_estimate=cost(4e6, 7e6),
    )(q.reshape(4, PANELS, GR, 128))


def update(rows_in, base, parts, last, xh, xl):
    strip = pl.BlockSpec(
        (pl.Element(GR), pl.Element(NCOL)), lambda g: (pl.multiple_of(WIN + g * GR, 16), 0)
    )
    spec = pl.BlockSpec((None, GR, SUB), lambda g: (g, 0, 0))
    return pl.pallas_call(
        update_kernel,
        grid=(GROUPS,),
        out_shape=jax.ShapeDtypeStruct((ROWS, NCOL), F32),
        in_specs=[spec] * 6 + [VM] * 4 + [strip, ANY],
        out_specs=strip,
        scratch_shapes=[pltpu.VMEM((GROUPS, GR, SUB), BF16)] * 2,
        input_output_aliases={11: 0},
        compiler_params=params(57),
        cost_estimate=cost(6 * TRAIL * DEPTH * NCOL, 30e6),
    )(*[v[0] for v in parts], *[v[1] for v in parts], *[v.reshape(2, PANELS, GR, 128) for v in last], xh, xl, rows_in, base)


def moved(arrays, shapes, plan, limit):
    def kernel(*refs):
        sems = refs[-1]
        outs = refs[len(arrays) : -1]
        copies = []
        for k, (i, take, o, put) in enumerate(plan):
            src = refs[i] if take is None else refs[i].at[take]
            dst = outs[o] if put is None else outs[o].at[put]
            copies.append(pltpu.make_async_copy(src, dst, sems.at[k]))
        for copy in copies:
            copy.start()
        for copy in copies:
            copy.wait()

    return pl.pallas_call(
        kernel,
        out_shape=[jax.ShapeDtypeStruct(v, F32) for v in shapes],
        in_specs=[ANY] * len(arrays),
        out_specs=[VM] * len(shapes),
        scratch_shapes=[pltpu.SemaphoreType.DMA((len(plan),))],
        compiler_params=params(limit),
    )(*arrays)


def second_hop(hop, *after):
    (kept,) = moved(
        (hop, along_y(hop[:1]), *after),
        [(3, *hop.shape[1:])],
        [(0, None, 0, pl.ds(0, 2)), (1, None, 0, pl.ds(2, 1))],
        30,
    )
    return kept, from_core(kept)


def local(rhs_tile, factor):
    row_i, col_i = lax.axis_index("row"), lax.axis_index("col")
    pos = jnp.stack([row_i // 2, row_i % 2, col_i // NZ, col_i % NZ]).astype(jnp.int32)

    packed = pl.pallas_call(
        pack_kernel,
        out_shape=jax.ShapeDtypeStruct((WR + PANELS * GR, 128), F32),
        in_specs=[VM],
        out_specs=VM,
        compiler_params=params(8),
    )(factor)
    rows3 = (PANELS, PB, NCOL)
    (b0,) = moved(
        (rhs_tile,),
        [rows3],
        [(0, pl.ds(p * PB, PB), 0, p) for p in range(PANELS)],
        55,
    )
    bc = from_core(b0)
    (bpair,) = moved((b0, bc, packed), [(2, *rows3)], [(0, None, 0, 0), (1, None, 0, 1)], 8)
    bhop = along_y(bpair)

    u1, u3 = from_first(packed, 1), from_first(packed, 3)
    total = WR + PANELS * GR
    h = WR + PANELS * GR // 2
    f1, f3 = moved(
        (u1, u3),
        [(h, 128), (total - h, 128)],
        [(0, pl.ds(0, h), 0, None), (1, pl.ds(h, total - h), 1, None)],
        8,
    )
    o1, o3 = from_first(f1, 1), from_first(f3, 3)

    half = h - WR
    w1, q0 = moved(
        (packed, u1, o1, u3, o3, bhop),
        [(4, WR, 128), (4, total - WR, 128)],
        [(j, pl.ds(0, WR), 0, j) for j in range(4)]
        + [(j, pl.ds(WR, total - WR), 1, j) for j in (0, 1, 3)]
        + [
            (2, pl.ds(WR, half), 1, (2, pl.ds(0, half))),
            (4, None, 1, (2, pl.ds(half, half))),
        ],
        16,
    )
    groups = [w1] + [from_second(w1, d) for d in (1, 2, 3)]
    q1, q3 = from_second(q0, 1), from_second(q0, 3)
    q2 = (from_second(q1[:2], 1), from_second(q3[2:], 3))

    mine = pl.pallas_call(
        rows_kernel,
        out_shape=jax.ShapeDtypeStruct((SLOTS, PB, PANEL), F32),
        in_specs=[SM] + [VM] * 4,
        out_specs=VM,
        scratch_shapes=[
            pltpu.VMEM((16, 2 * PB, 128), F32),
            pltpu.VMEM((PANELS, NX, PB, 128), F32),
        ],
        compiler_params=params(8),
    )(pos, *groups)

    mc = from_core(mine)
    rows = (mine, mc, *second_hop(along_y(jnp.stack([mine, mc])), q1, q3))
    rhs_rows = (b0, bc, *second_hop(bhop))

    parts = [assemble(q0), assemble(q1), assemble(q3)]
    xh, xl, base = pl.pallas_call(
        solve_kernel,
        out_shape=(
            jax.ShapeDtypeStruct((DEPTH, NCOL), BF16),
            jax.ShapeDtypeStruct((DEPTH, NCOL), BF16),
            jax.ShapeDtypeStruct((ROWS, NCOL), F32),
        ),
        in_specs=[SM] + [ANY] * 8,
        out_specs=(VM, VM, ANY),
        scratch_shapes=[
            pltpu.VMEM((SLOTS, PANEL, PANEL), F32),
            pltpu.VMEM((PANELS, PANEL, NCOL), F32),
        ]
        + [pltpu.VMEM((PANELS, PANEL, PANEL), BF16)] * 4
        + [pltpu.VMEM((PANEL, NCOL), BF16)] * 2
        + [pltpu.VMEM((DEPTH, NCOL), BF16)] * 2
        + [
            pltpu.VMEM((PANEL, NCOL), F32),
            pltpu.VMEM((WIN, NCOL), F32),
            pltpu.SemaphoreType.DMA((2, 2 * NY)),
            pltpu.SemaphoreType.DMA,
        ],
        compiler_params=params(42),
        cost_estimate=cost(36 * PANEL * PANEL * NCOL, 20e6),
    )(pos, *rows, *rhs_rows)

    return update(rhs_tile, base, parts, q2, xh, xl)


def solution(mesh):
    spec = P("row", "col")
    return jax.shard_map(
        local, mesh=mesh, in_specs=(spec, spec), out_specs=spec, check_vma=False
    )
```

```python
import jax
import jax.numpy as jnp
from jax import lax
from jax.experimental import pallas as pl
from jax.experimental.pallas import tpu as pltpu
from jax.sharding import PartitionSpec as P

F32, BF16 = jnp.float32, jnp.bfloat16
NX, NY, NZ = 4, 4, 4
ROWS, NCOL = 2304, 1152
PB, CB, PANEL, PANELS = 64, 32, 512, 3
WIN = PB * PANELS
TRAIL = ROWS - WIN
GROUPS = 4
GR = TRAIL // GROUPS
SLOTS = 6
WR = 2 * PB
SUB = PANELS * 128
CHUNK = GR // 3
MIB = 1024 * 1024
GROUP_ORDER = (0, 1, 3, 2)


def joint(v, dest):
    pairs = []
    for y in range(NY):
        for c in range(2):
            for x in range(NX):
                for z in range(NZ):
                    ty, tc, tx, tz = dest(y, c, x, z)
                    pairs.append(
                        (
                            (y * 2 + c) * 16 + x * 4 + z,
                            ((ty % NY) * 2 + tc % 2) * 16 + (tx % NX) * 4 + tz % NZ,
                        )
                    )
    return lax.ppermute(v, ("row", "col"), pairs)


def from_first(v, d):
    return joint(v, lambda y, c, x, z: (y, c, x - d, z) if c == 0 else (y, c, x, z - d))


def from_second(v, d):
    return joint(v, lambda y, c, x, z: (y, c, x, z - d) if c == 0 else (y, c, x - d, z))


def along_y(v):
    return joint(v, lambda y, c, x, z: (y - 1 if c == 0 else y + 1, c, x, z))


def from_core(v):
    return joint(v, lambda y, c, x, z: (y, 1 - c, x, z))


def pack_kernel(f_ref, l_ref):
    for p in range(PANELS):
        l_ref[WR + p * GR : WR + (p + 1) * GR, :] = jnp.concatenate(
            [
                f_ref[WIN + g * GR : WIN + (g + 1) * GR, p * CB : (p + 1) * CB]
                for g in range(GROUPS)
            ],
            axis=1,
        )

    def block(i, j):
        return f_ref[i * PB : (i + 1) * PB, j * CB : (j + 1) * CB]

    l_ref[0:PB, :] = jnp.concatenate([block(0, 0), block(1, 1), block(2, 2), block(1, 0)], axis=1)
    zero = jnp.zeros((PB, CB), F32)
    l_ref[PB:WR, :] = jnp.concatenate([block(2, 0), block(2, 1), zero, zero], axis=1)


def source(pos, i, j):
    core, x, z = pos[1], pos[2], pos[3]
    xs = jnp.where(core == 0, x + j, x + i) % NX
    zs = jnp.where(core == 0, z + i, z + j) % NZ
    return xs * NZ + zs


def rows_kernel(pos, g0, g1, g2, g3, out, canon, diag):
    y, core = pos[0], pos[1]
    for i, ref in enumerate((g0, g1, g2, g3)):
        for j in range(4):
            canon[source(pos, i, j)] = ref[j]
    lane = lax.broadcasted_iota(jnp.int32, (PB, 128), 1)
    row = lax.broadcasted_iota(jnp.int32, (PB, 128), 0)
    for s in range(SLOTS):
        half, q = divmod(s, 4)
        for xs in range(NX):
            total = None
            for zs in range(NZ):
                v = canon[xs * NZ + zs, half * PB : (half + 1) * PB, :]
                shift = (zs - q) % 4 * CB
                v = pltpu.roll(v, shift, 1) if shift else v
                total = v if total is None else jnp.where(lane // CB == zs, v, total)
            out[s, :, xs * 128 : (xs + 1) * 128] = total
            if s < PANELS:
                diag[s, xs] = total
    eye = (lane == row).astype(F32)
    blocks, mats, sols = [], [], []
    for p in range(PANELS):
        blk = diag[p, y]
        blocks.append(blk)
        a = jnp.where(core == 1, pltpu.roll(blk, PB, 1), blk)
        mats.append((a, a - eye))
        sols.append([eye[8 * k : 8 * k + 8] for k in range(PB // 8)])
    for i in range(PB):
        for p in range(PANELS):
            a, am = mats[p]
            k0, r0 = divmod(i, 8)
            top = sols[p][k0][r0 : r0 + 1, :] * (1.0 / a[i : i + 1, i : i + 1])
            for k in range(k0, PB // 8):
                sols[p][k] = sols[p][k] - am[8 * k : 8 * k + 8, i : i + 1] * top
    for p in range(PANELS):
        inv = jnp.concatenate(sols[p], axis=0)
        inv = jnp.where(core == 1, pltpu.roll(inv, PB, 1), inv)
        inv = jnp.where(lane // PB == core, inv, blocks[p])
        for k in range(NY):

            @pl.when(y == k)
            def _(p=p, k=k, inv=inv):
                out[p, :, k * 128 : (k + 1) * 128] = inv


def exact_dot(a, b):
    return jnp.dot(a, b, precision=lax.Precision.HIGHEST, preferred_element_type=F32)


def split(v):
    hi = v.astype(BF16)
    return hi, (v - hi.astype(F32)).astype(BF16)


def dot3(a, b):
    return jnp.dot(
        jnp.concatenate([a[0], a[0], a[1]], axis=1),
        jnp.concatenate([b[0], b[1], b[0]], axis=0),
        preferred_element_type=F32,
    )


COLS = [slice(c, min(c + 256, NCOL)) for c in range(0, NCOL, 256)]


def solve_kernel(
    pos, m0, mc, mown, mgot, b0, bc, bown, bgot, xh, xl, base, mat, b_ref, lh, ll, oh, ol, rh, rl, ah, al, xs, own, sem, last
):
    y, core = pos[0], pos[1]

    near, far = 1 + 2 * core, 3 - 2 * core

    def copies(to, own_rows, pair_rows, own3, got3, sems):
        made = []
        plan = (
            (own_rows, 0, core),
            (pair_rows, 0, 1 - core),
            (own3.at[0], near, core),
            (own3.at[1], near, 1 - core),
            (own3.at[2], 2, core),
            (got3.at[0], far, 1 - core),
            (got3.at[1], far, core),
            (got3.at[2], 2, 1 - core),
        )
        for k, (src, d, c) in enumerate(plan):
            r = pl.multiple_of((y + d) % NY * 128 + c * PB, PB)
            made.append(pltpu.make_async_copy(src, to.at[:, pl.ds(r, PB), :], sems.at[k]))
        return made

    mat_copies = copies(mat, m0, mc, mown, mgot, sem.at[0])
    b_copies = copies(b_ref, b0, bc, bown, bgot, sem.at[1])
    for copy in mat_copies + b_copies:
        copy.start()
    for copy in mat_copies:
        copy.wait()

    row = lax.broadcasted_iota(jnp.int32, (128, 128), 0) // PB
    col = lax.broadcasted_iota(jnp.int32, (128, 128), 1) // PB
    inv = {}
    for p in range(PANELS):
        for b in range(4):
            blk = mat[p, b * 128 : (b + 1) * 128, b * 128 : (b + 1) * 128]
            diag = jnp.where(row == col, blk, 0.0)
            low = jnp.where(row > col, blk, 0.0)
            inv[p, b] = diag - exact_dot(diag, exact_dot(low, diag))
    for p in range(PANELS):
        for b in range(4):
            mat[p, b * 128 : (b + 1) * 128, b * 128 : (b + 1) * 128] = inv[p, b]
    for size in (128, 256):
        for p in range(PANELS):
            for b in range(0, PANEL // size, 2):
                lo, mid, hi = b * size, (b + 1) * size, (b + 2) * size
                off = exact_dot(
                    mat[p, mid:hi, mid:hi],
                    exact_dot(mat[p, mid:hi, lo:mid], mat[p, lo:mid, lo:mid]),
                )
                mat[p, mid:hi, lo:mid] = -off
    for p in range(PANELS):
        lh[p], ll[p] = split(mat[p])
        oh[p], ol[p] = split(mat[PANELS + p])

    for copy in b_copies:
        copy.wait()
    left = {1: (0,), 2: (1, 2)}
    half = PANEL // 2
    for p in range(PANELS):
        for w in COLS:
            rhs = b_ref[p, :, w]
            if p:
                o = [jnp.concatenate([v[k] for k in left[p]], axis=1) for v in (oh, ol)]
                rhs = rhs - dot3(o, [v[: p * PANEL, w] for v in (ah, al)])
            rh[:, w], rl[:, w] = split(rhs)
        for w in COLS:
            for top, depth in ((0, half), (half, PANEL)):
                x = dot3(
                    [v[p, top : top + half, :depth] for v in (lh, ll)],
                    [v[:depth, w] for v in (rh, rl)],
                )
                part = slice(p * PANEL + top, p * PANEL + top + half)
                xs[top : top + half, w] = x
                ah[part, w], al[part, w] = split(x)
        mine_rows = pl.multiple_of((y * 2 + core) * PB, PB)
        own[p * PB : (p + 1) * PB, :] = xs[pl.ds(mine_rows, PB), :]
        for k, i in enumerate(GROUP_ORDER):
            for j in range(4):
                src = pl.multiple_of(p * PANEL + source(pos, i, j) * CB, CB)
                dst = (k * PANELS + p) * 128 + j * CB
                xh[dst : dst + CB, :] = ah[pl.ds(src, CB), :]
                xl[dst : dst + CB, :] = al[pl.ds(src, CB), :]
    copy = pltpu.make_async_copy(own, base.at[0:WIN, :], last)
    copy.start()
    copy.wait()


def lanes_in_order(block, rows, lh, ll):
    lane = lax.broadcasted_iota(jnp.int32, (rows.size, 128), 1)
    low64 = lane < 64
    low32 = lane % 64 < 32
    for p in range(PANELS):
        v = [block(j, p) for j in range(4)]
        for j in range(2):
            a, b = v[j], v[j + 2]
            v[j] = jnp.where(low64, a, pltpu.roll(b, 64, 1))
            v[j + 2] = jnp.where(low64, pltpu.roll(a, 64, 1), b)
        for j in (0, 2):
            a, b = v[j], v[j + 1]
            v[j] = jnp.where(low32, a, pltpu.roll(b, 32, 1))
            v[j + 1] = jnp.where(low32, pltpu.roll(a, 96, 1), b)
        for g in range(GROUPS):
            k = slice(p * 128, (p + 1) * 128)
            lh[g, rows, k], ll[g, rows, k] = split(v[g])


def assemble_kernel(q, lh, ll):
    lanes_in_order(lambda j, p: q[j, p], pl.ds(0, CHUNK), lh, ll)


def update_kernel(*refs):
    his, los, (qa, qb, xh, xl, r_ref, _base, out, lh, ll) = refs[:3], refs[3:6], refs[6:]
    g = pl.program_id(0)

    @pl.when(g == 0)
    def _():
        @pl.loop(0, GR // CHUNK)
        def _(i):
            rows = pl.ds(pl.multiple_of(i * CHUNK, 16), CHUNK)
            lanes_in_order(lambda j, p: (qa, qb)[j // 2][j % 2, p, rows, :], rows, lh, ll)

    a = [
        jnp.concatenate([v[...] for v in part] + [last[g]], axis=1)
        for part, last in ((his, lh), (los, ll))
    ]
    for w in COLS:
        out[:, w] = r_ref[:, w] - dot3(a, (xh[:, w], xl[:, w]))


VM = pl.BlockSpec(memory_space=pltpu.VMEM)
SM = pl.BlockSpec(memory_space=pltpu.SMEM)
ANY = pl.BlockSpec(memory_space=pl.ANY)
DEPTH = PANELS * PANEL


def params(limit):
    return pltpu.CompilerParams(vmem_limit_bytes=limit * MIB)


def cost(flops, moved):
    return pl.CostEstimate(flops=int(flops), bytes_accessed=int(moved), transcendentals=0)


def assemble(q):
    out = jax.ShapeDtypeStruct((GROUPS, GR, SUB), BF16)
    spec = pl.BlockSpec((GROUPS, CHUNK, SUB), lambda i: (0, i, 0))
    return pl.pallas_call(
        assemble_kernel,
        grid=(GR // CHUNK,),
        out_shape=(out, out),
        in_specs=[pl.BlockSpec((4, PANELS, CHUNK, 128), lambda i: (0, 0, i, 0))],
        out_specs=(spec, spec),
        compiler_params=params(12),
        cost_estimate=cost(4e6, 7e6),
    )(q.reshape(4, PANELS, GR, 128))


def update(rows_in, base, parts, last, xh, xl):
    strip = pl.BlockSpec(
        (pl.Element(GR), pl.Element(NCOL)), lambda g: (pl.multiple_of(WIN + g * GR, 16), 0)
    )
    spec = pl.BlockSpec((None, GR, SUB), lambda g: (g, 0, 0))
    return pl.pallas_call(
        update_kernel,
        grid=(GROUPS,),
        out_shape=jax.ShapeDtypeStruct((ROWS, NCOL), F32),
        in_specs=[spec] * 6 + [VM] * 4 + [strip, ANY],
        out_specs=strip,
        scratch_shapes=[pltpu.VMEM((GROUPS, GR, SUB), BF16)] * 2,
        input_output_aliases={11: 0},
        compiler_params=params(57),
        cost_estimate=cost(6 * TRAIL * DEPTH * NCOL, 30e6),
    )(*[v[0] for v in parts], *[v[1] for v in parts], *[v.reshape(2, PANELS, GR, 128) for v in last], xh, xl, rows_in, base)


def moved(arrays, shapes, plan, limit):
    def kernel(*refs):
        sems = refs[-1]
        outs = refs[len(arrays) : -1]
        copies = []
        for k, (i, take, o, put) in enumerate(plan):
            src = refs[i] if take is None else refs[i].at[take]
            dst = outs[o] if put is None else outs[o].at[put]
            copies.append(pltpu.make_async_copy(src, dst, sems.at[k]))
        for copy in copies:
            copy.start()
        for copy in copies:
            copy.wait()

    return pl.pallas_call(
        kernel,
        out_shape=[jax.ShapeDtypeStruct(v, F32) for v in shapes],
        in_specs=[ANY] * len(arrays),
        out_specs=[VM] * len(shapes),
        scratch_shapes=[pltpu.SemaphoreType.DMA((len(plan),))],
        compiler_params=params(limit),
    )(*arrays)


def second_hop(hop, early=(), late=()):
    shape = (1, *hop.shape[1:])
    (first,) = moved((hop, *early), [shape], [(0, pl.ds(0, 1), 0, None)], 30)
    (kept,) = moved(
        (hop, along_y(first), *late),
        [(3, *hop.shape[1:])],
        [(0, None, 0, pl.ds(0, 2)), (1, None, 0, pl.ds(2, 1))],
        30,
    )
    return kept, from_core(kept)


def local(rhs_tile, factor):
    row_i, col_i = lax.axis_index("row"), lax.axis_index("col")
    pos = jnp.stack([row_i // 2, row_i % 2, col_i // NZ, col_i % NZ]).astype(jnp.int32)

    packed = pl.pallas_call(
        pack_kernel,
        out_shape=jax.ShapeDtypeStruct((WR + PANELS * GR, 128), F32),
        in_specs=[VM],
        out_specs=VM,
        compiler_params=params(8),
    )(factor)
    rows3 = (PANELS, PB, NCOL)
    (b0,) = moved(
        (rhs_tile,),
        [rows3],
        [(0, pl.ds(p * PB, PB), 0, p) for p in range(PANELS)],
        55,
    )
    bc = from_core(b0)
    (bpair,) = moved((b0, bc, packed), [(2, *rows3)], [(0, None, 0, 0), (1, None, 0, 1)], 8)
    bhop = along_y(bpair)

    u1, u3 = from_first(packed, 1), from_first(packed, 3)
    total = WR + PANELS * GR
    h = WR + PANELS * GR // 2
    f1, f3 = moved(
        (u1, u3),
        [(h, 128), (total - h, 128)],
        [(0, pl.ds(0, h), 0, None), (1, pl.ds(h, total - h), 1, None)],
        8,
    )
    o1, o3 = from_first(f1, 1), from_first(f3, 3)

    half = h - WR
    w1, q0 = moved(
        (packed, u1, o1, u3, o3, bhop),
        [(4, WR, 128), (4, total - WR, 128)],
        [(j, pl.ds(0, WR), 0, j) for j in range(4)]
        + [(j, pl.ds(WR, total - WR), 1, j) for j in (0, 1, 3)]
        + [
            (2, pl.ds(WR, half), 1, (2, pl.ds(0, half))),
            (4, None, 1, (2, pl.ds(half, half))),
        ],
        16,
    )
    groups = [w1] + [from_second(w1, d) for d in (1, 2, 3)]
    q1, q3 = from_second(q0, 1), from_second(q0, 3)
    q2 = (from_second(q1[:2], 1), from_second(q3[2:], 3))

    mine = pl.pallas_call(
        rows_kernel,
        out_shape=jax.ShapeDtypeStruct((SLOTS, PB, PANEL), F32),
        in_specs=[SM] + [VM] * 4,
        out_specs=VM,
        scratch_shapes=[
            pltpu.VMEM((16, 2 * PB, 128), F32),
            pltpu.VMEM((PANELS, NX, PB, 128), F32),
        ],
        compiler_params=params(8),
    )(pos, *groups)

    parts = [assemble(q0), assemble(q1), assemble(q3)]
    mc = from_core(mine)
    early = (q1, q3, parts[0][0])
    late = (parts[1][0], parts[2][0])
    rows = (mine, mc, *second_hop(along_y(jnp.stack([mine, mc])), early, late))
    rhs_rows = (b0, bc, *second_hop(bhop))

    xh, xl, base = pl.pallas_call(
        solve_kernel,
        out_shape=(
            jax.ShapeDtypeStruct((DEPTH, NCOL), BF16),
            jax.ShapeDtypeStruct((DEPTH, NCOL), BF16),
            jax.ShapeDtypeStruct((ROWS, NCOL), F32),
        ),
        in_specs=[SM] + [ANY] * 8,
        out_specs=(VM, VM, ANY),
        scratch_shapes=[
            pltpu.VMEM((SLOTS, PANEL, PANEL), F32),
            pltpu.VMEM((PANELS, PANEL, NCOL), F32),
        ]
        + [pltpu.VMEM((PANELS, PANEL, PANEL), BF16)] * 4
        + [pltpu.VMEM((PANEL, NCOL), BF16)] * 2
        + [pltpu.VMEM((DEPTH, NCOL), BF16)] * 2
        + [
            pltpu.VMEM((PANEL, NCOL), F32),
            pltpu.VMEM((WIN, NCOL), F32),
            pltpu.SemaphoreType.DMA((2, 2 * NY)),
            pltpu.SemaphoreType.DMA,
        ],
        compiler_params=params(42),
        cost_estimate=cost(36 * PANEL * PANEL * NCOL, 20e6),
    )(pos, *rows, *rhs_rows)

    return update(rhs_tile, base, parts, q2, xh, xl)


def solution(mesh):
    spec = P("row", "col")
    return jax.shard_map(
        local, mesh=mesh, in_specs=(spec, spec), out_specs=spec, check_vma=False
    )
```

```python
import jax
import jax.numpy as jnp
from jax import lax
from jax.experimental import pallas as pl
from jax.experimental.pallas import tpu as pltpu
from jax.sharding import PartitionSpec as P

F32, BF16 = jnp.float32, jnp.bfloat16
NX, NY, NZ = 4, 4, 4
ROWS, NCOL = 2304, 1152
PB, CB, PANEL, PANELS = 64, 32, 512, 3
WIN = PB * PANELS
TRAIL = ROWS - WIN
GROUPS = 4
GR = TRAIL // GROUPS
SLOTS = 6
WR = 2 * PB
SUB = PANELS * 128
CHUNK = GR // 3
MIB = 1024 * 1024
GROUP_ORDER = (0, 1, 3, 2)


def joint(v, dest):
    pairs = []
    for y in range(NY):
        for c in range(2):
            for x in range(NX):
                for z in range(NZ):
                    ty, tc, tx, tz = dest(y, c, x, z)
                    pairs.append(
                        (
                            (y * 2 + c) * 16 + x * 4 + z,
                            ((ty % NY) * 2 + tc % 2) * 16 + (tx % NX) * 4 + tz % NZ,
                        )
                    )
    return lax.ppermute(v, ("row", "col"), pairs)


def from_first(v, d):
    return joint(v, lambda y, c, x, z: (y, c, x - d, z) if c == 0 else (y, c, x, z - d))


def from_second(v, d):
    return joint(v, lambda y, c, x, z: (y, c, x, z - d) if c == 0 else (y, c, x - d, z))


def along_y(v):
    return joint(v, lambda y, c, x, z: (y - 1 if c == 0 else y + 1, c, x, z))


def from_core(v):
    return joint(v, lambda y, c, x, z: (y, 1 - c, x, z))


def pack_kernel(f_ref, l_ref, w_ref):
    for p in range(PANELS):
        l_ref[p * GR : (p + 1) * GR, :] = jnp.concatenate(
            [
                f_ref[WIN + g * GR : WIN + (g + 1) * GR, p * CB : (p + 1) * CB]
                for g in range(GROUPS)
            ],
            axis=1,
        )

    def block(i, j):
        return f_ref[i * PB : (i + 1) * PB, j * CB : (j + 1) * CB]

    w_ref[0:PB, :] = jnp.concatenate([block(0, 0), block(1, 1), block(2, 2), block(1, 0)], axis=1)
    zero = jnp.zeros((PB, CB), F32)
    w_ref[PB:WR, :] = jnp.concatenate([block(2, 0), block(2, 1), zero, zero], axis=1)


def source(pos, i, j):
    core, x, z = pos[1], pos[2], pos[3]
    xs = jnp.where(core == 0, x + j, x + i) % NX
    zs = jnp.where(core == 0, z + i, z + j) % NZ
    return xs * NZ + zs


def rows_kernel(pos, g0, g1, g2, g3, _after, out, canon, diag):
    y, core = pos[0], pos[1]
    for i, ref in enumerate((g0, g1, g2, g3)):
        for j in range(4):
            canon[source(pos, i, j)] = ref[j]
    lane = lax.broadcasted_iota(jnp.int32, (PB, 128), 1)
    row = lax.broadcasted_iota(jnp.int32, (PB, 128), 0)
    for s in range(SLOTS):
        half, q = divmod(s, 4)
        for xs in range(NX):
            total = None
            for zs in range(NZ):
                v = canon[xs * NZ + zs, half * PB : (half + 1) * PB, :]
                shift = (zs - q) % 4 * CB
                v = pltpu.roll(v, shift, 1) if shift else v
                total = v if total is None else jnp.where(lane // CB == zs, v, total)
            out[s, :, xs * 128 : (xs + 1) * 128] = total
            if s < PANELS:
                diag[s, xs] = total
    eye = (lane == row).astype(F32)
    blocks, mats, sols = [], [], []
    for p in range(PANELS):
        blk = diag[p, y]
        blocks.append(blk)
        a = jnp.where(core == 1, pltpu.roll(blk, PB, 1), blk)
        mats.append((a, a - eye))
        sols.append([eye[8 * k : 8 * k + 8] for k in range(PB // 8)])
    for i in range(PB):
        for p in range(PANELS):
            a, am = mats[p]
            k0, r0 = divmod(i, 8)
            top = sols[p][k0][r0 : r0 + 1, :] * (1.0 / a[i : i + 1, i : i + 1])
            for k in range(k0, PB // 8):
                sols[p][k] = sols[p][k] - am[8 * k : 8 * k + 8, i : i + 1] * top
    for p in range(PANELS):
        inv = jnp.concatenate(sols[p], axis=0)
        inv = jnp.where(core == 1, pltpu.roll(inv, PB, 1), inv)
        inv = jnp.where(lane // PB == core, inv, blocks[p])
        for k in range(NY):

            @pl.when(y == k)
            def _(p=p, k=k, inv=inv):
                out[p, :, k * 128 : (k + 1) * 128] = inv


def exact_dot(a, b):
    return jnp.dot(a, b, precision=lax.Precision.HIGHEST, preferred_element_type=F32)


def split(v):
    hi = v.astype(BF16)
    return hi, (v - hi.astype(F32)).astype(BF16)


def dot3(a, b):
    return jnp.dot(
        jnp.concatenate([a[0], a[0], a[1]], axis=1),
        jnp.concatenate([b[0], b[1], b[0]], axis=0),
        preferred_element_type=F32,
    )


COLS = [slice(c, min(c + 256, NCOL)) for c in range(0, NCOL, 256)]


def solve_kernel(
    pos, m0, mc, mown, mgot, b0, bc, bown, bgot, xh, xl, base, mat, b_ref, lh, ll, oh, ol, rh, rl, ah, al, xs, own, sem, last
):
    y, core = pos[0], pos[1]

    near, far = 1 + 2 * core, 3 - 2 * core

    def copies(to, own_rows, pair_rows, own3, got3, sems):
        made = []
        plan = (
            (own_rows, 0, core),
            (pair_rows, 0, 1 - core),
            (own3.at[0], near, core),
            (own3.at[1], near, 1 - core),
            (own3.at[2], 2, core),
            (got3.at[0], far, 1 - core),
            (got3.at[1], far, core),
            (got3.at[2], 2, 1 - core),
        )
        for k, (src, d, c) in enumerate(plan):
            r = pl.multiple_of((y + d) % NY * 128 + c * PB, PB)
            made.append(pltpu.make_async_copy(src, to.at[:, pl.ds(r, PB), :], sems.at[k]))
        return made

    mat_copies = copies(mat, m0, mc, mown, mgot, sem.at[0])
    b_copies = copies(b_ref, b0, bc, bown, bgot, sem.at[1])
    for copy in mat_copies + b_copies:
        copy.start()
    for copy in mat_copies:
        copy.wait()

    row = lax.broadcasted_iota(jnp.int32, (128, 128), 0) // PB
    col = lax.broadcasted_iota(jnp.int32, (128, 128), 1) // PB
    inv = {}
    for p in range(PANELS):
        for b in range(4):
            blk = mat[p, b * 128 : (b + 1) * 128, b * 128 : (b + 1) * 128]
            diag = jnp.where(row == col, blk, 0.0)
            low = jnp.where(row > col, blk, 0.0)
            inv[p, b] = diag - exact_dot(diag, exact_dot(low, diag))
    for p in range(PANELS):
        for b in range(4):
            mat[p, b * 128 : (b + 1) * 128, b * 128 : (b + 1) * 128] = inv[p, b]
    for size in (128, 256):
        for p in range(PANELS):
            for b in range(0, PANEL // size, 2):
                lo, mid, hi = b * size, (b + 1) * size, (b + 2) * size
                off = exact_dot(
                    mat[p, mid:hi, mid:hi],
                    exact_dot(mat[p, mid:hi, lo:mid], mat[p, lo:mid, lo:mid]),
                )
                mat[p, mid:hi, lo:mid] = -off
    for p in range(PANELS):
        lh[p], ll[p] = split(mat[p])
        oh[p], ol[p] = split(mat[PANELS + p])

    for copy in b_copies:
        copy.wait()
    left = {1: (0,), 2: (1, 2)}
    half = PANEL // 2
    for p in range(PANELS):
        for w in COLS:
            rhs = b_ref[p, :, w]
            if p:
                o = [jnp.concatenate([v[k] for k in left[p]], axis=1) for v in (oh, ol)]
                rhs = rhs - dot3(o, [v[: p * PANEL, w] for v in (ah, al)])
            rh[:, w], rl[:, w] = split(rhs)
        for w in COLS:
            for top, depth in ((0, half), (half, PANEL)):
                x = dot3(
                    [v[p, top : top + half, :depth] for v in (lh, ll)],
                    [v[:depth, w] for v in (rh, rl)],
                )
                part = slice(p * PANEL + top, p * PANEL + top + half)
                xs[top : top + half, w] = x
                ah[part, w], al[part, w] = split(x)
        mine_rows = pl.multiple_of((y * 2 + core) * PB, PB)
        own[p * PB : (p + 1) * PB, :] = xs[pl.ds(mine_rows, PB), :]
        for k, i in enumerate(GROUP_ORDER):
            for j in range(4):
                src = pl.multiple_of(p * PANEL + source(pos, i, j) * CB, CB)
                dst = (k * PANELS + p) * 128 + j * CB
                xh[dst : dst + CB, :] = ah[pl.ds(src, CB), :]
                xl[dst : dst + CB, :] = al[pl.ds(src, CB), :]
    copy = pltpu.make_async_copy(own, base.at[0:WIN, :], last)
    copy.start()
    copy.wait()


def lanes_in_order(block, rows, lh, ll):
    lane = lax.broadcasted_iota(jnp.int32, (rows.size, 128), 1)
    low64 = lane < 64
    low32 = lane % 64 < 32
    for p in range(PANELS):
        v = [block(j, p) for j in range(4)]
        for j in range(2):
            a, b = v[j], v[j + 2]
            v[j] = jnp.where(low64, a, pltpu.roll(b, 64, 1))
            v[j + 2] = jnp.where(low64, pltpu.roll(a, 64, 1), b)
        for j in (0, 2):
            a, b = v[j], v[j + 1]
            v[j] = jnp.where(low32, a, pltpu.roll(b, 32, 1))
            v[j + 1] = jnp.where(low32, pltpu.roll(a, 96, 1), b)
        for g in range(GROUPS):
            k = slice(p * 128, (p + 1) * 128)
            lh[g, rows, k], ll[g, rows, k] = split(v[g])


def assemble_kernel(q, *refs):
    lanes_in_order(lambda j, p: q[j, p], pl.ds(0, CHUNK), *refs[-2:])


def update_kernel(*refs):
    his, los, (xh, xl, r_ref, _base, out) = refs[:3], refs[3:6], refs[6:]
    a = [jnp.concatenate([v[...] for v in part], axis=1) for part in (his, los)]
    for w in COLS:
        out[:, w] = r_ref[:, w] - dot3(a, (xh[:, w], xl[:, w]))


def update_last_kernel(qa, qb, xh, xl, r_ref, out, lh, ll):
    g = pl.program_id(0)

    @pl.when(g == 0)
    def _():
        @pl.loop(0, GR // CHUNK)
        def _(i):
            rows = pl.ds(pl.multiple_of(i * CHUNK, 16), CHUNK)
            lanes_in_order(lambda j, p: (qa, qb)[j // 2][j % 2, p, rows, :], rows, lh, ll)

    for w in COLS:
        out[:, w] = r_ref[:, w] - dot3((lh[g], ll[g]), (xh[:, w], xl[:, w]))


VM = pl.BlockSpec(memory_space=pltpu.VMEM)
SM = pl.BlockSpec(memory_space=pltpu.SMEM)
ANY = pl.BlockSpec(memory_space=pl.ANY)
DEPTH = PANELS * PANEL


def params(limit):
    return pltpu.CompilerParams(vmem_limit_bytes=limit * MIB)


def cost(flops, moved):
    return pl.CostEstimate(flops=int(flops), bytes_accessed=int(moved), transcendentals=0)


def assemble(q, *after):
    out = jax.ShapeDtypeStruct((GROUPS, GR, SUB), BF16)
    spec = pl.BlockSpec((GROUPS, CHUNK, SUB), lambda i: (0, i, 0))
    return pl.pallas_call(
        assemble_kernel,
        grid=(GR // CHUNK,),
        out_shape=(out, out),
        in_specs=[pl.BlockSpec((4, PANELS, CHUNK, 128), lambda i: (0, 0, i, 0))]
        + [ANY] * len(after),
        out_specs=(spec, spec),
        compiler_params=params(12),
        cost_estimate=cost(4e6, 7e6),
    )(q.reshape(4, PANELS, GR, 128), *after)


STRIP = pl.BlockSpec(
    (pl.Element(GR), pl.Element(NCOL)), lambda g: (pl.multiple_of(WIN + g * GR, 16), 0)
)


def update(rows_in, base, parts, xh, xl):
    spec = pl.BlockSpec((None, GR, SUB), lambda g: (g, 0, 0))
    xs = pl.BlockSpec((3 * SUB, NCOL), lambda g: (0, 0))
    return pl.pallas_call(
        update_kernel,
        grid=(GROUPS,),
        out_shape=jax.ShapeDtypeStruct((ROWS, NCOL), F32),
        in_specs=[spec] * 6 + [xs, xs, STRIP, ANY],
        out_specs=STRIP,
        input_output_aliases={9: 0},
        compiler_params=params(48),
        cost_estimate=cost(6 * TRAIL * 3 * SUB * NCOL, 30e6),
    )(*[v[0] for v in parts], *[v[1] for v in parts], xh, xl, rows_in, base)


def update_last(base, last, xh, xl):
    xs = pl.BlockSpec((SUB, NCOL), lambda g: (3, 0))
    return pl.pallas_call(
        update_last_kernel,
        grid=(GROUPS,),
        out_shape=jax.ShapeDtypeStruct((ROWS, NCOL), F32),
        in_specs=[VM, VM, xs, xs, STRIP],
        out_specs=STRIP,
        scratch_shapes=[pltpu.VMEM((GROUPS, GR, SUB), BF16)] * 2,
        input_output_aliases={4: 0},
        compiler_params=params(48),
        cost_estimate=cost(6 * TRAIL * SUB * NCOL, 25e6),
    )(*[v.reshape(2, PANELS, GR, 128) for v in last], xh, xl, base)


def moved(arrays, shapes, plan, limit):
    def kernel(*refs):
        sems = refs[-1]
        outs = refs[len(arrays) : -1]
        copies = []
        for k, (i, take, o, put) in enumerate(plan):
            src = refs[i] if take is None else refs[i].at[take]
            dst = outs[o] if put is None else outs[o].at[put]
            copies.append(pltpu.make_async_copy(src, dst, sems.at[k]))
        for copy in copies:
            copy.start()
        for copy in copies:
            copy.wait()

    return pl.pallas_call(
        kernel,
        out_shape=[jax.ShapeDtypeStruct(v, F32) for v in shapes],
        in_specs=[ANY] * len(arrays),
        out_specs=[VM] * len(shapes),
        scratch_shapes=[pltpu.SemaphoreType.DMA((len(plan),))],
        compiler_params=params(limit),
    )(*arrays)


def second_hop(hop, early=(), late=()):
    shape = (1, *hop.shape[1:])
    (first,) = moved((hop, *early), [shape], [(0, pl.ds(0, 1), 0, None)], 30)
    (kept,) = moved(
        (hop, along_y(first), *late),
        [(3, *hop.shape[1:])],
        [(0, None, 0, pl.ds(0, 2)), (1, None, 0, pl.ds(2, 1))],
        30,
    )
    return kept, from_core(kept)


def local(rhs_tile, factor):
    row_i, col_i = lax.axis_index("row"), lax.axis_index("col")
    pos = jnp.stack([row_i // 2, row_i % 2, col_i // NZ, col_i % NZ]).astype(jnp.int32)

    packed, w = pl.pallas_call(
        pack_kernel,
        out_shape=(
            jax.ShapeDtypeStruct((PANELS * GR, 128), F32),
            jax.ShapeDtypeStruct((WR, 128), F32),
        ),
        in_specs=[VM],
        out_specs=(VM, VM),
        compiler_params=params(8),
    )(factor)
    rows3 = (PANELS, PB, NCOL)
    (b0,) = moved(
        (rhs_tile,),
        [rows3],
        [(0, pl.ds(p * PB, PB), 0, p) for p in range(PANELS)],
        55,
    )
    bc = from_core(b0)
    (bpair,) = moved((b0, bc, packed), [(2, *rows3)], [(0, None, 0, 0), (1, None, 0, 1)], 8)
    bhop = along_y(bpair)

    (w1,) = moved(
        (w, *[from_first(w, d) for d in (1, 2, 3)], bpair),
        [(4, WR, 128)],
        [(j, None, 0, j) for j in range(4)],
        8,
    )
    groups = [w1] + [from_second(w1, d) for d in (1, 2, 3)]

    total = PANELS * GR
    h = total // 2
    (packed,) = moved((packed, *groups[1:]), [(total, 128)], [(0, None, 0, None)], 8)
    u1, u3 = from_first(packed, 1), from_first(packed, 3)
    f1, f3 = moved(
        (u1, u3),
        [(h, 128), (h, 128)],
        [(0, pl.ds(0, h), 0, None), (1, pl.ds(h, h), 1, None)],
        8,
    )
    o1, o3 = from_first(f1, 1), from_first(f3, 3)
    (q0,) = moved(
        (packed, u1, o1, u3, o3),
        [(4, total, 128)],
        [
            (0, None, 0, 0),
            (1, None, 0, 1),
            (2, None, 0, (2, pl.ds(0, h))),
            (3, None, 0, 3),
            (4, None, 0, (2, pl.ds(h, h))),
        ],
        16,
    )
    q1, q3 = from_second(q0, 1), from_second(q0, 3)

    mine = pl.pallas_call(
        rows_kernel,
        out_shape=jax.ShapeDtypeStruct((SLOTS, PB, PANEL), F32),
        in_specs=[SM] + [VM] * 4 + [ANY],
        out_specs=VM,
        scratch_shapes=[
            pltpu.VMEM((16, 2 * PB, 128), F32),
            pltpu.VMEM((PANELS, NX, PB, 128), F32),
        ],
        compiler_params=params(8),
    )(pos, *groups, bhop)

    mc = from_core(mine)
    first = assemble(q0)
    rows = (mine, mc, *second_hop(along_y(jnp.stack([mine, mc])), late=(first[0],)))
    rhs_rows = (b0, bc, *second_hop(bhop))

    xh, xl, base = pl.pallas_call(
        solve_kernel,
        out_shape=(
            jax.ShapeDtypeStruct((DEPTH, NCOL), BF16),
            jax.ShapeDtypeStruct((DEPTH, NCOL), BF16),
            jax.ShapeDtypeStruct((ROWS, NCOL), F32),
        ),
        in_specs=[SM] + [ANY] * 8,
        out_specs=(VM, VM, ANY),
        scratch_shapes=[
            pltpu.VMEM((SLOTS, PANEL, PANEL), F32),
            pltpu.VMEM((PANELS, PANEL, NCOL), F32),
        ]
        + [pltpu.VMEM((PANELS, PANEL, PANEL), BF16)] * 4
        + [pltpu.VMEM((PANEL, NCOL), BF16)] * 2
        + [pltpu.VMEM((DEPTH, NCOL), BF16)] * 2
        + [
            pltpu.VMEM((PANEL, NCOL), F32),
            pltpu.VMEM((WIN, NCOL), F32),
            pltpu.SemaphoreType.DMA((2, 2 * NY)),
            pltpu.SemaphoreType.DMA,
        ],
        compiler_params=params(42),
        cost_estimate=cost(1e6, 1e6),
    )(pos, *rows, *rhs_rows)

    f1, f3 = moved(
        (q1, q3, xh),
        [(2, total, 128), (2, total, 128)],
        [(0, pl.ds(0, 2), 0, None), (1, pl.ds(2, 2), 1, None)],
        16,
    )
    q2 = (from_second(f1, 1), from_second(f3, 3))
    parts = [first, assemble(q1, xh), assemble(q3, xh)]
    base = update(rhs_tile, base, parts, xh, xl)
    return update_last(base, q2, xh, xl)


def solution(mesh):
    spec = P("row", "col")
    return jax.shard_map(
        local, mesh=mesh, in_specs=(spec, spec), out_specs=spec, check_vma=False
    )
```

```python
import jax
import jax.numpy as jnp
from jax import lax
from jax.experimental import pallas as pl
from jax.experimental.pallas import tpu as pltpu
from jax.sharding import PartitionSpec as P

F32, BF16 = jnp.float32, jnp.bfloat16
NX, NY, NZ = 4, 4, 4
ROWS, NCOL = 2304, 1152
PB, CB, PANEL, PANELS = 64, 32, 512, 3
WIN = PB * PANELS
TRAIL = ROWS - WIN
GROUPS = 4
GR = TRAIL // GROUPS
SLOTS = 6
WR = 2 * PB
SUB = PANELS * 128
CHUNK = GR // 3
MIB = 1024 * 1024
GROUP_ORDER = (0, 1, 3, 2)


def joint(v, dest):
    pairs = []
    for y in range(NY):
        for c in range(2):
            for x in range(NX):
                for z in range(NZ):
                    ty, tc, tx, tz = dest(y, c, x, z)
                    pairs.append(
                        (
                            (y * 2 + c) * 16 + x * 4 + z,
                            ((ty % NY) * 2 + tc % 2) * 16 + (tx % NX) * 4 + tz % NZ,
                        )
                    )
    return lax.ppermute(v, ("row", "col"), pairs)


def from_first(v, d):
    return joint(v, lambda y, c, x, z: (y, c, x - d, z) if c == 0 else (y, c, x, z - d))


def from_second(v, d):
    return joint(v, lambda y, c, x, z: (y, c, x, z - d) if c == 0 else (y, c, x - d, z))


def along_y(v):
    return joint(v, lambda y, c, x, z: (y - 1 if c == 0 else y + 1, c, x, z))


def from_core(v):
    return joint(v, lambda y, c, x, z: (y, 1 - c, x, z))


def pack_kernel(f_ref, l_ref, w_ref):
    for p in range(PANELS):
        l_ref[p * GR : (p + 1) * GR, :] = jnp.concatenate(
            [
                f_ref[WIN + g * GR : WIN + (g + 1) * GR, p * CB : (p + 1) * CB]
                for g in range(GROUPS)
            ],
            axis=1,
        )

    def block(i, j):
        return f_ref[i * PB : (i + 1) * PB, j * CB : (j + 1) * CB]

    w_ref[0:PB, :] = jnp.concatenate([block(0, 0), block(1, 1), block(2, 2), block(1, 0)], axis=1)
    zero = jnp.zeros((PB, CB), F32)
    w_ref[PB:WR, :] = jnp.concatenate([block(2, 0), block(2, 1), zero, zero], axis=1)


def source(pos, i, j):
    core, x, z = pos[1], pos[2], pos[3]
    xs = jnp.where(core == 0, x + j, x + i) % NX
    zs = jnp.where(core == 0, z + i, z + j) % NZ
    return xs * NZ + zs


def rows_kernel(pos, g0, g1, g2, g3, _hop, _packed, out, canon, diag):
    y, core = pos[0], pos[1]
    for i, ref in enumerate((g0, g1, g2, g3)):
        for j in range(4):
            canon[source(pos, i, j)] = ref[j]
    lane = lax.broadcasted_iota(jnp.int32, (PB, 128), 1)
    row = lax.broadcasted_iota(jnp.int32, (PB, 128), 0)
    for s in range(SLOTS):
        half, q = divmod(s, 4)
        for xs in range(NX):
            total = None
            for zs in range(NZ):
                v = canon[xs * NZ + zs, half * PB : (half + 1) * PB, :]
                shift = (zs - q) % 4 * CB
                v = pltpu.roll(v, shift, 1) if shift else v
                total = v if total is None else jnp.where(lane // CB == zs, v, total)
            out[s, :, xs * 128 : (xs + 1) * 128] = total
            if s < PANELS:
                diag[s, xs] = total
    eye = (lane == row).astype(F32)
    blocks, mats, sols = [], [], []
    for p in range(PANELS):
        blk = diag[p, y]
        blocks.append(blk)
        a = jnp.where(core == 1, pltpu.roll(blk, PB, 1), blk)
        mats.append((a, a - eye))
        sols.append([eye[8 * k : 8 * k + 8] for k in range(PB // 8)])
    for i in range(PB):
        for p in range(PANELS):
            a, am = mats[p]
            k0, r0 = divmod(i, 8)
            top = sols[p][k0][r0 : r0 + 1, :] * (1.0 / a[i : i + 1, i : i + 1])
            for k in range(k0, PB // 8):
                sols[p][k] = sols[p][k] - am[8 * k : 8 * k + 8, i : i + 1] * top
    for p in range(PANELS):
        inv = jnp.concatenate(sols[p], axis=0)
        inv = jnp.where(core == 1, pltpu.roll(inv, PB, 1), inv)
        inv = jnp.where(lane // PB == core, inv, blocks[p])
        for k in range(NY):

            @pl.when(y == k)
            def _(p=p, k=k, inv=inv):
                out[p, :, k * 128 : (k + 1) * 128] = inv


def exact_dot(a, b):
    return jnp.dot(a, b, precision=lax.Precision.HIGHEST, preferred_element_type=F32)


def split(v):
    hi = v.astype(BF16)
    return hi, (v - hi.astype(F32)).astype(BF16)


def dot3(a, b):
    return jnp.dot(
        jnp.concatenate([a[0], a[0], a[1]], axis=1),
        jnp.concatenate([b[0], b[1], b[0]], axis=0),
        preferred_element_type=F32,
    )


COLS = [slice(c, min(c + 256, NCOL)) for c in range(0, NCOL, 256)]


def solve_kernel(
    pos, m0, mc, mown, mgot, b0, bc, bown, bgot, xh, xl, base, token, mat, b_ref, lh, ll, oh, ol, rh, rl, ah, al, xs, own, sem, last
):
    y, core = pos[0], pos[1]

    near, far = 1 + 2 * core, 3 - 2 * core

    def copies(to, own_rows, pair_rows, own3, got3, sems):
        made = []
        plan = (
            (own_rows, 0, core),
            (pair_rows, 0, 1 - core),
            (own3.at[0], near, core),
            (own3.at[1], near, 1 - core),
            (own3.at[2], 2, core),
            (got3.at[0], far, 1 - core),
            (got3.at[1], far, core),
            (got3.at[2], 2, 1 - core),
        )
        for k, (src, d, c) in enumerate(plan):
            r = pl.multiple_of((y + d) % NY * 128 + c * PB, PB)
            made.append(pltpu.make_async_copy(src, to.at[:, pl.ds(r, PB), :], sems.at[k]))
        return made

    mat_copies = copies(mat, m0, mc, mown, mgot, sem.at[0])
    b_copies = copies(b_ref, b0, bc, bown, bgot, sem.at[1])
    for copy in mat_copies + b_copies:
        copy.start()
    for copy in mat_copies:
        copy.wait()

    row = lax.broadcasted_iota(jnp.int32, (128, 128), 0) // PB
    col = lax.broadcasted_iota(jnp.int32, (128, 128), 1) // PB
    inv = {}
    for p in range(PANELS):
        for b in range(4):
            blk = mat[p, b * 128 : (b + 1) * 128, b * 128 : (b + 1) * 128]
            diag = jnp.where(row == col, blk, 0.0)
            low = jnp.where(row > col, blk, 0.0)
            inv[p, b] = diag - exact_dot(diag, exact_dot(low, diag))
    for p in range(PANELS):
        for b in range(4):
            mat[p, b * 128 : (b + 1) * 128, b * 128 : (b + 1) * 128] = inv[p, b]
    for size in (128, 256):
        for p in range(PANELS):
            for b in range(0, PANEL // size, 2):
                lo, mid, hi = b * size, (b + 1) * size, (b + 2) * size
                off = exact_dot(
                    mat[p, mid:hi, mid:hi],
                    exact_dot(mat[p, mid:hi, lo:mid], mat[p, lo:mid, lo:mid]),
                )
                mat[p, mid:hi, lo:mid] = -off
    for p in range(PANELS):
        lh[p], ll[p] = split(mat[p])
        oh[p], ol[p] = split(mat[PANELS + p])

    for copy in b_copies:
        copy.wait()
    left = {1: (0,), 2: (1, 2)}
    half = PANEL // 2
    for p in range(PANELS):
        for w in COLS:
            rhs = b_ref[p, :, w]
            if p:
                o = [jnp.concatenate([v[k] for k in left[p]], axis=1) for v in (oh, ol)]
                rhs = rhs - dot3(o, [v[: p * PANEL, w] for v in (ah, al)])
            rh[:, w], rl[:, w] = split(rhs)
        for w in COLS:
            for top, depth in ((0, half), (half, PANEL)):
                x = dot3(
                    [v[p, top : top + half, :depth] for v in (lh, ll)],
                    [v[:depth, w] for v in (rh, rl)],
                )
                part = slice(p * PANEL + top, p * PANEL + top + half)
                xs[top : top + half, w] = x
                ah[part, w], al[part, w] = split(x)
        mine_rows = pl.multiple_of((y * 2 + core) * PB, PB)
        own[p * PB : (p + 1) * PB, :] = xs[pl.ds(mine_rows, PB), :]
        for k, i in enumerate(GROUP_ORDER):
            for j in range(4):
                src = pl.multiple_of(p * PANEL + source(pos, i, j) * CB, CB)
                dst = (k * PANELS + p) * 128 + j * CB
                xh[dst : dst + CB, :] = ah[pl.ds(src, CB), :]
                xl[dst : dst + CB, :] = al[pl.ds(src, CB), :]
    token[...] = xs[0:8, 0:128]
    copy = pltpu.make_async_copy(own, base.at[0:WIN, :], last)
    copy.start()
    copy.wait()


def lanes_in_order(block, rows, lh, ll):
    lane = lax.broadcasted_iota(jnp.int32, (rows.size, 128), 1)
    low64 = lane < 64
    low32 = lane % 64 < 32
    for p in range(PANELS):
        v = [block(j, p) for j in range(4)]
        for j in range(2):
            a, b = v[j], v[j + 2]
            v[j] = jnp.where(low64, a, pltpu.roll(b, 64, 1))
            v[j + 2] = jnp.where(low64, pltpu.roll(a, 64, 1), b)
        for j in (0, 2):
            a, b = v[j], v[j + 1]
            v[j] = jnp.where(low32, a, pltpu.roll(b, 32, 1))
            v[j + 1] = jnp.where(low32, pltpu.roll(a, 96, 1), b)
        for g in range(GROUPS):
            k = slice(p * 128, (p + 1) * 128)
            lh[g, rows, k], ll[g, rows, k] = split(v[g])


def assemble_kernel(q, *refs):
    lanes_in_order(lambda j, p: q[j, p], pl.ds(0, CHUNK), *refs[-2:])


def update_kernel(*refs):
    his, los, (xh, xl, r_ref, _base, out) = refs[:3], refs[3:6], refs[6:]
    a = [jnp.concatenate([v[...] for v in part], axis=1) for part in (his, los)]
    for w in COLS:
        out[:, w] = r_ref[:, w] - dot3(a, (xh[:, w], xl[:, w]))


def update_last_kernel(qa, qb, xh, xl, r_ref, out, lh, ll):
    g = pl.program_id(0)

    @pl.when(g == 0)
    def _():
        @pl.loop(0, GR // CHUNK)
        def _(i):
            rows = pl.ds(pl.multiple_of(i * CHUNK, 16), CHUNK)
            lanes_in_order(lambda j, p: (qa, qb)[j // 2][j % 2, p, rows, :], rows, lh, ll)

    for w in COLS:
        out[:, w] = r_ref[:, w] - dot3((lh[g], ll[g]), (xh[:, w], xl[:, w]))


VM = pl.BlockSpec(memory_space=pltpu.VMEM)
SM = pl.BlockSpec(memory_space=pltpu.SMEM)
ANY = pl.BlockSpec(memory_space=pl.ANY)
DEPTH = PANELS * PANEL


def params(limit):
    return pltpu.CompilerParams(vmem_limit_bytes=limit * MIB)


def cost(flops, moved):
    return pl.CostEstimate(flops=int(flops), bytes_accessed=int(moved), transcendentals=0)


def assemble(q, *after):
    out = jax.ShapeDtypeStruct((GROUPS, GR, SUB), BF16)
    spec = pl.BlockSpec((GROUPS, CHUNK, SUB), lambda i: (0, i, 0))
    return pl.pallas_call(
        assemble_kernel,
        grid=(GR // CHUNK,),
        out_shape=(out, out),
        in_specs=[pl.BlockSpec((4, PANELS, CHUNK, 128), lambda i: (0, 0, i, 0))]
        + [ANY] * len(after),
        out_specs=(spec, spec),
        compiler_params=params(12),
        cost_estimate=cost(4e6, 7e6),
    )(q.reshape(4, PANELS, GR, 128), *after)


STRIP = pl.BlockSpec(
    (pl.Element(GR), pl.Element(NCOL)), lambda g: (pl.multiple_of(WIN + g * GR, 16), 0)
)


def update(rows_in, base, parts, xh, xl):
    spec = pl.BlockSpec((None, GR, SUB), lambda g: (g, 0, 0))
    xs = pl.BlockSpec((3 * SUB, NCOL), lambda g: (0, 0))
    return pl.pallas_call(
        update_kernel,
        grid=(GROUPS,),
        out_shape=jax.ShapeDtypeStruct((ROWS, NCOL), F32),
        in_specs=[spec] * 6 + [xs, xs, STRIP, ANY],
        out_specs=STRIP,
        input_output_aliases={9: 0},
        compiler_params=params(57),
        cost_estimate=cost(6 * TRAIL * 3 * SUB * NCOL, 30e6),
    )(*[v[0] for v in parts], *[v[1] for v in parts], xh, xl, rows_in, base)


def update_last(base, last, xh, xl):
    xs = pl.BlockSpec((SUB, NCOL), lambda g: (3, 0))
    return pl.pallas_call(
        update_last_kernel,
        grid=(GROUPS,),
        out_shape=jax.ShapeDtypeStruct((ROWS, NCOL), F32),
        in_specs=[VM, VM, xs, xs, STRIP],
        out_specs=STRIP,
        scratch_shapes=[pltpu.VMEM((GROUPS, GR, SUB), BF16)] * 2,
        input_output_aliases={4: 0},
        compiler_params=params(57),
        cost_estimate=cost(6 * TRAIL * SUB * NCOL, 25e6),
    )(*[v.reshape(2, PANELS, GR, 128) for v in last], xh, xl, base)


def moved(arrays, shapes, plan, limit):
    def kernel(*refs):
        sems = refs[-1]
        outs = refs[len(arrays) : -1]
        copies = []
        for k, (i, take, o, put) in enumerate(plan):
            src = refs[i] if take is None else refs[i].at[take]
            dst = outs[o] if put is None else outs[o].at[put]
            copies.append(pltpu.make_async_copy(src, dst, sems.at[k]))
        for copy in copies:
            copy.start()
        for copy in copies:
            copy.wait()

    return pl.pallas_call(
        kernel,
        out_shape=[jax.ShapeDtypeStruct(v, F32) for v in shapes],
        in_specs=[ANY] * len(arrays),
        out_specs=[VM] * len(shapes),
        scratch_shapes=[pltpu.SemaphoreType.DMA((len(plan),))],
        compiler_params=params(limit),
    )(*arrays)


def joined(hop, hop2):
    (kept,) = moved(
        (hop, hop2),
        [(3, *hop.shape[1:])],
        [(0, None, 0, pl.ds(0, 2)), (1, None, 0, pl.ds(2, 1))],
        30,
    )
    return kept, from_core(kept)


def local(rhs_tile, factor):
    row_i, col_i = lax.axis_index("row"), lax.axis_index("col")
    pos = jnp.stack([row_i // 2, row_i % 2, col_i // NZ, col_i % NZ]).astype(jnp.int32)

    packed, w = pl.pallas_call(
        pack_kernel,
        out_shape=(
            jax.ShapeDtypeStruct((PANELS * GR, 128), F32),
            jax.ShapeDtypeStruct((WR, 128), F32),
        ),
        in_specs=[VM],
        out_specs=(VM, VM),
        compiler_params=params(8),
    )(factor)
    rows3 = (PANELS, PB, NCOL)
    (b0,) = moved(
        (rhs_tile,),
        [rows3],
        [(0, pl.ds(p * PB, PB), 0, p) for p in range(PANELS)],
        55,
    )
    bc = from_core(b0)
    (bpair,) = moved((b0, bc, packed), [(2, *rows3)], [(0, None, 0, 0), (1, None, 0, 1)], 8)
    bhop = along_y(bpair)

    (w1,) = moved(
        (w, *[from_first(w, d) for d in (1, 2, 3)], bpair),
        [(4, WR, 128)],
        [(j, None, 0, j) for j in range(4)],
        8,
    )
    groups = [w1] + [from_second(w1, d) for d in (1, 2, 3)]

    total = PANELS * GR
    h = total // 2
    (packed,) = moved((packed, *groups[1:]), [(total, 128)], [(0, None, 0, None)], 8)
    mine = pl.pallas_call(
        rows_kernel,
        out_shape=jax.ShapeDtypeStruct((SLOTS, PB, PANEL), F32),
        in_specs=[SM] + [VM] * 4 + [ANY] * 2,
        out_specs=VM,
        scratch_shapes=[
            pltpu.VMEM((16, 2 * PB, 128), F32),
            pltpu.VMEM((PANELS, NX, PB, 128), F32),
        ],
        compiler_params=params(8),
    )(pos, *groups, bhop, packed)

    mc = from_core(mine)
    (bfirst,) = moved((bhop,), [(1, *rows3)], [(0, pl.ds(0, 1), 0, None)], 8)
    bhop2 = along_y(bfirst)
    tile = (SLOTS, PB, PANEL)
    (wpair,) = moved((mine, mc, bhop2), [(2, *tile)], [(0, None, 0, 0), (1, None, 0, 1)], 16)
    whop = along_y(wpair)

    u1, u3 = from_first(packed, 1), from_first(packed, 3)
    f1, f3, wfirst = moved(
        (u1, u3, whop),
        [(h, 128), (h, 128), (1, *tile)],
        [
            (0, pl.ds(0, h), 0, None),
            (1, pl.ds(h, h), 1, None),
            (2, pl.ds(0, 1), 2, None),
        ],
        8,
    )
    whop2 = along_y(wfirst)
    o1, o3 = from_first(f1, 1), from_first(f3, 3)
    (q0,) = moved(
        (packed, u1, o1, u3, o3, whop2),
        [(4, total, 128)],
        [
            (0, None, 0, 0),
            (1, None, 0, 1),
            (2, None, 0, (2, pl.ds(0, h))),
            (3, None, 0, 3),
            (4, None, 0, (2, pl.ds(h, h))),
        ],
        16,
    )
    q1, q3 = from_second(q0, 1), from_second(q0, 3)

    first = assemble(q0)
    rows = (mine, mc, *joined(whop, whop2))
    rhs_rows = (b0, bc, *joined(bhop, bhop2))

    xh, xl, base, token = pl.pallas_call(
        solve_kernel,
        out_shape=(
            jax.ShapeDtypeStruct((DEPTH, NCOL), BF16),
            jax.ShapeDtypeStruct((DEPTH, NCOL), BF16),
            jax.ShapeDtypeStruct((ROWS, NCOL), F32),
            jax.ShapeDtypeStruct((8, 128), F32),
        ),
        in_specs=[SM] + [ANY] * 8,
        out_specs=(VM, VM, ANY, VM),
        scratch_shapes=[
            pltpu.VMEM((SLOTS, PANEL, PANEL), F32),
            pltpu.VMEM((PANELS, PANEL, NCOL), F32),
        ]
        + [pltpu.VMEM((PANELS, PANEL, PANEL), BF16)] * 4
        + [pltpu.VMEM((PANEL, NCOL), BF16)] * 2
        + [pltpu.VMEM((DEPTH, NCOL), BF16)] * 2
        + [
            pltpu.VMEM((PANEL, NCOL), F32),
            pltpu.VMEM((WIN, NCOL), F32),
            pltpu.SemaphoreType.DMA((2, 2 * NY)),
            pltpu.SemaphoreType.DMA,
        ],
        compiler_params=params(42),
        cost_estimate=cost(1e6, 1e6),
    )(pos, *rows, *rhs_rows)

    f1, f3 = moved(
        (q1, q3, token),
        [(2, total, 128), (2, total, 128)],
        [(0, pl.ds(0, 2), 0, None), (1, pl.ds(2, 2), 1, None)],
        16,
    )
    q2 = (from_second(f1, 1), from_second(f3, 3))
    parts = [first, assemble(q1, token), assemble(q3, token)]
    base = update(rhs_tile, base, parts, xh, xl)
    return update_last(base, q2, xh, xl)


def solution(mesh):
    spec = P("row", "col")
    return jax.shard_map(
        local, mesh=mesh, in_specs=(spec, spec), out_specs=spec, check_vma=False
    )
```
